256 devices in a mesh: scene: 16 (over z_hi, x), view: 16 (over y, z_lo, core).
Axes of the slice: x: 4, y: 4, z: 8 (z_hi: 4, z_lo: 2; z = z_hi * 2 + z_lo), core: 2. Of those that a mesh axis runs over, the one named last changes fastest.
Arguments:
- keys: bfloat16 [32768, 1024], P(('scene', 'view')), parts along dimension 0, may hold values from -6 to 6
- values: bfloat16 [32768, 1024], P(('scene', 'view')), parts along dimension 0, may hold values from -6 to 6
- rates: bfloat16 [32768, 16], P(('scene', 'view')), parts along dimension 0, may hold values from 0.099609375 to 1
- queries: bfloat16 [16384, 1024], P(('scene', 'view')), parts along dimension 0, may hold values from -6 to 6
- gate_up: bfloat16 [2, 16, 64, 1024], P(None, None, None, 'view'), may hold values from -0.75 to 0.75
- down_t: bfloat16 [16, 64, 1024], P(None, None, 'view'), may hold values from -0.1875 to 0.1875
- step_sizes: float32 [16], replicated, may hold values from 1 to 4
- gain: float32 [1024], replicated, may hold values from 0.1 to 1.9
Outputs:
- outputs: bfloat16 [16384, 1024], P(('scene', 'view')), parts along dimension 0
The draws below stay inside these ranges and needn't reach their ends.
There are 16 independent parts, one for each index of `scene`. The reference program is written for one: setup_inputs(seed, part) draws one part's arguments, and reference() takes and returns one part's arrays. A program takes and returns all parts, laid end to end along the dimension named above; an argument that names none is the same for every part. Nothing has to cross between parts.
All inputs are finite; a program needn't handle non-finite values.
Results may differ from the reference program's by a relative error of at most 0.0083.
Values may be sent and summed in bfloat16 or wider, within the bound.
A program may use at most 128 MiB of HBM per device.

```python
import math
import jax
import jax.numpy as jnp
from jax import lax

HEADS = 16
DH = 64
HID = 1024
D = 1024
NS_STEPS = 5
TOKENS = 2048
QUERIES = 1024


def levels(key, dims, pieces, least, largest):
    def one(axis_at, parts):
        heights = jax.random.uniform(jax.random.fold_in(jax.random.fold_in(key, 6), axis_at), (parts,), jnp.float32, least / len(pieces), largest / len(pieces))
        return jnp.repeat(jnp.exp(heights), dims[axis_at] // parts).reshape((-1,) + (1,) * (len(dims) - axis_at - 1))

    level = one(*pieces[0])
    for cut in pieces[1:]:
        level = level * one(*cut)
    return level


def scatter_about(key, shape, deviation, limit, split=(), dtype=jnp.bfloat16):
    entries = deviation * jax.random.normal(key, shape, jnp.float32)
    if split:
        entries = entries * levels(key, shape, split, -0.22, 0.18)
    return jnp.clip(entries, -limit, limit).astype(dtype)


def setup_inputs(seed: int = 0, part: int = 0) -> dict:
    key_of = jax.random.split(jax.random.key(seed), 9)
    own_keys = jax.random.split(jax.random.fold_in(key_of[8], part), 9)
    return {
        "keys": scatter_about(own_keys[0], (TOKENS, D), 1.0, 6.0, ((0, 16),)),
        "values": scatter_about(own_keys[1], (TOKENS, D), 1.0, 6.0, ((0, 16),)),
        "rates": jnp.clip(jnp.exp(math.log(1.0) - 2.306499 * jax.random.uniform(own_keys[2], (TOKENS, HEADS), jnp.float32) ** levels(own_keys[2], (TOKENS, HEADS), ((0, 16),), -0.2, 0.2)), 0.099609375, 1.0).astype(jnp.bfloat16),
        "queries": scatter_about(own_keys[3], (QUERIES, D), 1.0, 6.0, ((0, 16),)),
        "gate_up": scatter_about(key_of[4], (2, HEADS, DH, HID), DH ** -0.5, 0.75, ((3, 16),)),
        "down_t": scatter_about(key_of[5], (HEADS, DH, HID), HID ** -0.5, 0.1875, ((2, 16),)),
        "step_sizes": jnp.clip(jnp.exp(jax.random.uniform(key_of[6], (HEADS,), jnp.float32, math.log(1.0), math.log(4.0))), 1.0, 4.0),
        "gain": jnp.clip(1.0 + 0.18 * jax.random.normal(key_of[7], (D,), jnp.float32), 0.1, 1.9),
    }


poly_one = 3.4445
poly_two = -4.775
poly_three = 2.0315

def orthogonalize(grads):
    total = jnp.sqrt(lax.optimization_barrier(jnp.sum(grads * grads, axis=(1, 2), keepdims=True)))
    current = grads / (total + 1e-07)
    for step in range(NS_STEPS):
        gram = jnp.einsum('mik,mjk->mij', current, current, precision=lax.Precision.HIGHEST)
        square = jnp.einsum('mij,mjk->mik', gram, gram, precision=lax.Precision.HIGHEST)
        blend = poly_two * gram + poly_three * square
        current = poly_one * current + jnp.einsum('mij,mjk->mik', blend, current, precision=lax.Precision.HIGHEST)
    return current

def head_pass(operands):
    key_rows, value_rows, head_rates, gate_w, up_w, down_w, head_step, query_rows, head_gain = operands
    pre_gate = jnp.dot(key_rows, gate_w, preferred_element_type=jnp.float32)
    pre_up = jnp.dot(key_rows, up_w, preferred_element_type=jnp.float32)
    sigma = jax.nn.sigmoid(pre_gate)
    gated = pre_gate * sigma
    hidden = (gated * pre_up).astype(jnp.bfloat16)
    out_grad = (-(head_rates.astype(jnp.float32)[:, None] * value_rows.astype(jnp.float32))).astype(jnp.bfloat16)
    down_grad = jnp.dot(out_grad.T, hidden, preferred_element_type=jnp.float32)
    hidden_grad = jnp.dot(out_grad, down_w, preferred_element_type=jnp.float32)
    gate_term = (hidden_grad * pre_up * sigma * (1.0 + pre_gate * (1.0 - sigma))).astype(jnp.bfloat16)
    up_term = (hidden_grad * gated).astype(jnp.bfloat16)
    gate_grad = jnp.dot(key_rows.T, gate_term, preferred_element_type=jnp.float32)
    up_grad = jnp.dot(key_rows.T, up_term, preferred_element_type=jnp.float32)
    grads = jnp.stack([gate_grad, up_grad, down_grad])
    weights = jnp.stack([gate_w, up_w, down_w]).astype(jnp.float32)
    moved = weights - head_step * orthogonalize(grads)
    keep = jnp.sqrt(lax.optimization_barrier(jnp.sum(weights * weights, axis=1, keepdims=True)))
    length = jnp.sqrt(lax.optimization_barrier(jnp.sum(moved * moved, axis=1, keepdims=True)))
    fresh = (moved * (keep / (length + 1e-06))).astype(jnp.bfloat16)
    query_gate = jnp.dot(query_rows, fresh[0], preferred_element_type=jnp.float32)
    query_up = jnp.dot(query_rows, fresh[1], preferred_element_type=jnp.float32)
    query_hidden = (query_gate * jax.nn.sigmoid(query_gate) * query_up).astype(jnp.bfloat16)
    head_out = jnp.dot(query_hidden, fresh[2].T, preferred_element_type=jnp.float32)
    mean_square = lax.optimization_barrier(jnp.mean(head_out * head_out, axis=-1, keepdims=True))
    return (head_out * lax.rsqrt(mean_square + 1e-06) * head_gain).astype(jnp.bfloat16)

def reference(keys, values, rates, queries, gate_up, down_t, step_sizes, gain):
    key_heads = keys.reshape(TOKENS, HEADS, DH).transpose(1, 0, 2)
    value_heads = values.reshape(TOKENS, HEADS, DH).transpose(1, 0, 2)
    query_heads = queries.reshape(QUERIES, HEADS, DH).transpose(1, 0, 2)
    result = lax.map(head_pass, (key_heads, value_heads, rates.T, gate_up[0], gate_up[1], down_t, step_sizes, query_heads, gain.reshape(HEADS, DH)))
    return result.transpose(1, 0, 2).reshape(QUERIES, HEADS * DH)
```

```python
import jax
import jax.numpy as jnp
from jax import lax
from jax.sharding import PartitionSpec as P

NS_STEPS = 5


poly_one = 3.4445
poly_two = -4.775
poly_three = 2.0315


def exact_dot(left, right):
    return jnp.einsum("mij,mjk->mik", left, right, precision=lax.Precision.HIGHEST)


def fast_dot(spec, left, right):
    return jnp.einsum(spec, left, right, preferred_element_type=jnp.float32)


def grad_terms(keys, out_grad, gate_w, up_w, down_w):
    pre_gate = fast_dot("td,df->tf", keys, gate_w)
    pre_up = fast_dot("td,df->tf", keys, up_w)
    sigma = jax.nn.sigmoid(pre_gate)
    gated = pre_gate * sigma
    hidden = (gated * pre_up).astype(jnp.bfloat16)
    down_grad = fast_dot("td,tf->df", out_grad, hidden)
    hidden_grad = fast_dot("td,df->tf", out_grad, down_w)
    gate_term = (hidden_grad * pre_up * sigma * (1.0 + pre_gate * (1.0 - sigma))).astype(
        jnp.bfloat16
    )
    up_term = (hidden_grad * gated).astype(jnp.bfloat16)
    gate_grad = fast_dot("td,tf->df", keys, gate_term)
    up_grad = fast_dot("td,tf->df", keys, up_term)
    return jnp.stack([gate_grad, up_grad, down_grad])


def orthogonalize(grads):
    gram = jnp.einsum("mik,mjk->mij", grads, grads, precision=lax.Precision.HIGHEST)
    square_norm = jnp.trace(gram, axis1=1, axis2=2)[:, None, None]
    factor = 1.0 / (jnp.sqrt(square_norm) + 1e-07)
    gram = gram * (factor * factor)
    eye = jnp.eye(gram.shape[1], dtype=jnp.float32)
    total = None
    for step in range(NS_STEPS):
        square = exact_dot(gram, gram)
        blend = poly_one * eye + poly_two * gram + poly_three * square
        total = blend if total is None else exact_dot(blend, total)
        if step < NS_STEPS - 1:
            gram = exact_dot(exact_dot(blend, gram), blend)
    return exact_dot(total * factor, grads)


def renew_weights(grads, stacked, head_step):
    weights = stacked.astype(jnp.float32)
    moved = weights - head_step * orthogonalize(grads)
    keep = jnp.sqrt(jnp.sum(weights * weights, axis=1, keepdims=True))
    length = jnp.sqrt(jnp.sum(moved * moved, axis=1, keepdims=True))
    return (moved * (keep / (length + 1e-06))).astype(jnp.bfloat16)


def apply_head(queries, fresh, gain):
    query_gate = fast_dot("td,df->tf", queries, fresh[0])
    query_up = fast_dot("td,df->tf", queries, fresh[1])
    query_hidden = (query_gate * jax.nn.sigmoid(query_gate) * query_up).astype(jnp.bfloat16)
    head_out = fast_dot("tf,df->td", query_hidden, fresh[2])
    mean_square = jnp.mean(head_out * head_out, axis=-1, keepdims=True)
    return (head_out * lax.rsqrt(mean_square + 1e-06) * gain).astype(jnp.bfloat16)


def to_heads(rows, heads):
    count = rows.shape[0]
    split = rows.reshape(count, heads, -1).transpose(1, 0, 2)
    moved = lax.all_to_all(split, "view", split_axis=0, concat_axis=0, tiled=True)
    return moved.reshape(heads * count, -1)


def shards(keys, values, rates, queries, gate_up, down_t, step_sizes, gain):
    heads = rates.shape[1]
    mine = lax.axis_index("view")
    value_heads = values.reshape(values.shape[0], heads, -1).astype(jnp.float32)
    out_grad = (-(rates.astype(jnp.float32)[:, :, None] * value_heads)).astype(jnp.bfloat16)
    stacked = jnp.concatenate([gate_up, down_t[None]], axis=0)
    stacked = lax.all_to_all(stacked, "view", split_axis=1, concat_axis=3, tiled=True)[:, 0]
    grads = grad_terms(
        to_heads(keys, heads),
        to_heads(out_grad.reshape(values.shape), heads),
        stacked[0],
        stacked[1],
        stacked[2],
    )
    fresh = renew_weights(grads, stacked, step_sizes[mine])
    head_gain = lax.dynamic_slice_in_dim(gain.reshape(heads, -1), mine, 1)
    result = apply_head(to_heads(queries, heads), fresh, head_gain)
    count = queries.shape[0]
    back = lax.all_to_all(
        result.reshape(heads, count, -1), "view", split_axis=0, concat_axis=0, tiled=True
    )
    return back.transpose(1, 0, 2).reshape(count, -1)


def solution(mesh):
    return jax.shard_map(
        shards,
        mesh=mesh,
        in_specs=(
            P(("scene", "view"), None),
            P(("scene", "view"), None),
            P(("scene", "view"), None),
            P(("scene", "view"), None),
            P(None, None, None, "view"),
            P(None, None, "view"),
            P(),
            P(),
        ),
        out_specs=P(("scene", "view"), None),
        check_vma=False,
    )
```

```python
import jax
import jax.numpy as jnp
from jax import lax
from jax.experimental import pallas as pl
from jax.experimental.pallas import tpu as pltpu
from jax.sharding import PartitionSpec as P

NS_STEPS = 5
GROUP = 16
DH = 64
HID = 1024
LANES = 128
BLOCK = 128

poly_one = 3.4445
poly_two = -4.775
poly_three = 2.0315

ROWS_BY_ROWS = (((1,), (1,)), ((), ()))
COLS_BY_COLS = (((0,), (0,)), ((), ()))


def nt_dot(left, right):
    return lax.dot_general(left, right, ROWS_BY_ROWS, preferred_element_type=jnp.float32)


def plain_dot(left, right):
    return jnp.dot(left, right, preferred_element_type=jnp.float32)


def exact_dot(left, right):
    return jnp.dot(
        left, right, precision=lax.Precision.HIGHEST, preferred_element_type=jnp.float32
    )


def flip(block):
    return block.T


def clear_grads(grad):
    grad[...] = jnp.zeros_like(grad)


def unpack_weights(source, recv_w, weight, query):
    turned = flip(recv_w[source])
    low = pl.ds(pl.multiple_of(source * DH, DH), DH)
    weight[0, low, :] = turned[:DH, :DH]
    weight[1, low, :] = turned[:DH, DH:]
    weight[2, low, :] = turned[DH:, :DH]
    query[low, :] = turned[DH:, DH:]


def grad_chunk(pair, recv_t, weight, grad):
    key_cols = recv_t[pair, :DH, :]
    err_cols = recv_t[pair, DH:, :]

    def one(at):
        rows = pl.ds(pl.multiple_of(at * BLOCK, BLOCK), BLOCK)
        gate = plain_dot(weight[0, rows, :], key_cols)
        up = plain_dot(weight[1, rows, :], key_cols)
        back = plain_dot(weight[2, rows, :], err_cols)
        sigma = 0.5 * jnp.tanh(0.5 * gate) + 0.5
        gated = gate * sigma
        hidden = (gated * up).astype(jnp.bfloat16)
        up_term = (back * gated).astype(jnp.bfloat16)
        gate_term = (back * up * (sigma + gated * (1.0 - sigma))).astype(jnp.bfloat16)
        grad[0, rows, :] += nt_dot(gate_term, key_cols)
        grad[1, rows, :] += nt_dot(up_term, key_cols)
        grad[2, rows, :] += nt_dot(hidden, err_cols)

    def loop_body(at, carry):
        one(at)
        return carry

    lax.fori_loop(0, HID // BLOCK, loop_body, 0, unroll=True)


def orthogonalizers(grad):
    grams, totals = [], []
    eye = (
        lax.broadcasted_iota(jnp.int32, (DH, DH), 0) == lax.broadcasted_iota(jnp.int32, (DH, DH), 1)
    ).astype(jnp.float32)
    for part in range(3):
        gram = lax.dot_general(
            grad[part],
            grad[part],
            COLS_BY_COLS,
            precision=lax.Precision.HIGHEST,
            preferred_element_type=jnp.float32,
        )
        square_norm = jnp.sum(gram * eye, axis=(0, 1), keepdims=True)
        factor = 1.0 / (jnp.sqrt(square_norm) + 1e-07)
        grams.append(gram * (factor * factor))
        totals.append(factor * eye)
    for step in range(NS_STEPS):
        squares = [exact_dot(gram, gram) for gram in grams]
        blends = [
            poly_one * eye + poly_two * gram + poly_three * square
            for gram, square in zip(grams, squares)
        ]
        totals = [
            blend * total[:1, :1] if step == 0 else exact_dot(blend, total)
            for blend, total in zip(blends, totals)
        ]
        if step < NS_STEPS - 1:
            cubes = [exact_dot(gram, square) for gram, square in zip(grams, squares)]
            halves = [
                poly_one * gram + poly_two * square + poly_three * cube
                for gram, square, cube in zip(grams, squares, cubes)
            ]
            grams = [exact_dot(half, blend) for half, blend in zip(halves, blends)]
    return totals


def renew(grad, weight, fresh, step_size):
    totals = orthogonalizers(grad)
    for part in range(3):
        start = weight[part].astype(jnp.float32)
        moved = start - step_size * exact_dot(grad[part], totals[part])
        keep = jnp.sum(start * start, axis=1, keepdims=True)
        length = jnp.sum(moved * moved, axis=1, keepdims=True)
        fresh[part] = (moved * (jnp.sqrt(keep) / (jnp.sqrt(length) + 1e-06))).astype(jnp.bfloat16)


QROWS = 256


def apply_block(at, query, fresh, gain, send_o):
    rows = pl.ds(pl.multiple_of(at * QROWS, QROWS), QROWS)
    block = query[rows, :]
    hidden = []
    for half in range(4):
        cols = pl.ds(half * 256, 256)
        gate = nt_dot(block, fresh[0, cols, :])
        up = nt_dot(block, fresh[1, cols, :])
        sigma = 0.5 * jnp.tanh(0.5 * gate) + 0.5
        hidden.append((gate * sigma * up).astype(jnp.bfloat16))
    head_out = plain_dot(jnp.concatenate(hidden, axis=1), fresh[2])
    mean_square = jnp.sum(head_out * head_out, axis=1, keepdims=True) * (1.0 / DH)
    done = head_out * lax.rsqrt(mean_square + 1e-06) * gain
    for piece in range(QROWS // DH):
        top = done[piece * DH : piece * DH + DH // 2]
        bottom = done[piece * DH + DH // 2 : (piece + 1) * DH]
        send_o[at * (QROWS // DH) + piece] = jnp.concatenate([top, bottom], axis=1).astype(
            jnp.bfloat16
        )


def turn_tokens(pair, keys, values, rate_rows, queries, turned_q, send_t):
    cols = pl.ds(pl.multiple_of(pair * LANES, LANES), LANES)
    turned_k = flip(keys[:, cols])
    turned_v = flip(values[:, cols]).astype(jnp.float32)
    for side in range(2):
        head = 2 * pair + side
        rate = rate_rows[pl.ds(head, 1), :]
        part = slice(side * DH, (side + 1) * DH)
        send_t[head, :DH, :] = turned_k[part]
        send_t[head, DH:, :] = (-(rate * turned_v[part])).astype(jnp.bfloat16)


def pack_weights(pair, queries, gate_up, down_t, send_w):
    cols = pl.ds(pl.multiple_of(pair * LANES, LANES), LANES)
    turned_q = flip(queries[:, cols])
    for side in range(2):
        head = 2 * pair + side
        send_w[head, :DH, :] = jnp.concatenate([gate_up[0, head], down_t[head]], axis=1)
        send_w[head, DH:, :] = jnp.concatenate(
            [gate_up[1, head], turned_q[side * DH : (side + 1) * DH]], axis=1
        )


def whole_kernel(
    keys,
    values,
    rates,
    queries,
    gate_up,
    down_t,
    step_sizes,
    gain_rows,
    outputs,
    send_w,
    recv_w,
    send_t,
    recv_t,
    send_o,
    recv_o,
    rate_rows,
    weight,
    query,
    grad,
    fresh,
    w_out,
    w_in,
    t_out,
    t_in,
    o_out,
    o_in,
    here,
):
    me = lax.axis_index("view")
    my_pair, my_side = me // 2, me % 2
    my_cols = pl.ds(pl.multiple_of(my_side * LANES, LANES), LANES)

    def peer(step):
        return lax.rem(me + step, GROUP)

    def loop(count, one, first=0):
        def loop_body(at, carry):
            one(at)
            return carry

        lax.fori_loop(first, count, loop_body, 0)

    barrier = pltpu.get_barrier_semaphore()

    def greet(step):
        pl.semaphore_signal(
            barrier,
            inc=1,
            device_id={"view": peer(step)},
            device_id_type=pl.DeviceIdType.MESH,
        )

    loop(GROUP, greet, 1)

    def w_copy(target, origin):
        return pltpu.make_async_remote_copy(
            src_ref=send_w.at[target],
            dst_ref=recv_w.at[origin],
            send_sem=w_out.at[target],
            recv_sem=w_in.at[origin],
            device_id={"view": target},
            device_id_type=pl.DeviceIdType.MESH,
        )

    def t_copy(target, origin):
        cols = pl.ds(pl.multiple_of(lax.rem(origin, 2) * LANES, LANES), LANES)
        return pltpu.make_async_remote_copy(
            src_ref=send_t.at[target],
            dst_ref=recv_t.at[lax.div(origin, 2), :, cols],
            send_sem=t_out.at[target],
            recv_sem=t_in.at[origin],
            device_id={"view": target},
            device_id_type=pl.DeviceIdType.MESH,
        )

    def o_copy(target, origin):
        return pltpu.make_async_remote_copy(
            src_ref=send_o.at[target],
            dst_ref=recv_o.at[origin],
            send_sem=o_out.at[target],
            recv_sem=o_in.at[origin],
            device_id={"view": target},
            device_id_type=pl.DeviceIdType.MESH,
        )

    loop(GROUP // 2, lambda pair: pack_weights(pair, queries, gate_up, down_t, send_w))
    pl.semaphore_wait(barrier, GROUP - 1)

    loop(GROUP, lambda step: w_copy(peer(step), me).start(), 1)
    rate_rows[...] = flip(rates[...].astype(jnp.float32))
    loop(
        GROUP // 2,
        lambda pair: turn_tokens(pair, keys, values, rate_rows, None, None, send_t),
    )
    loop(GROUP, lambda step: t_copy(peer(step), me).start(), 1)

    own_w = pltpu.make_async_copy(send_w.at[me], recv_w.at[me], here.at[0])
    own_t = pltpu.make_async_copy(send_t.at[me], recv_t.at[my_pair, :, my_cols], here.at[1])
    own_w.start()
    own_t.start()
    clear_grads(grad)
    own_w.wait()
    unpack_weights(me, recv_w, weight, query)

    def take_weights(step):
        origin = peer(GROUP - step)
        w_copy(origin, origin).wait_recv()
        unpack_weights(origin, recv_w, weight, query)

    loop(GROUP, take_weights, 1)
    own_t.wait()
    other = my_pair * 2 + 1 - my_side
    t_copy(other, other).wait_recv()
    grad_chunk(my_pair, recv_t, weight, grad)

    def take_tokens(step):
        pair = lax.rem(my_pair + GROUP // 2 - step, GROUP // 2)
        t_copy(2 * pair, 2 * pair).wait_recv()
        t_copy(2 * pair + 1, 2 * pair + 1).wait_recv()
        grad_chunk(pair, recv_t, weight, grad)

    loop(GROUP // 2, take_tokens, 1)

    renew(grad, weight, fresh, step_sizes[me])
    gain = gain_rows[pl.ds(my_pair, 1), :]
    gain = jnp.where(my_side == 0, gain[:, :DH], gain[:, DH:])

    for at in range(HID // QROWS):
        apply_block(at, query, fresh, gain, send_o)
        for target in range(at * (QROWS // DH), (at + 1) * (QROWS // DH)):

            @pl.when(target != me)
            def _():
                o_copy(target, me).start()

    own_o = pltpu.make_async_copy(send_o.at[me], recv_o.at[me], here.at[2])
    own_o.start()
    own_o.wait()

    def take_outputs(step):
        o_copy(peer(step), peer(step)).wait_recv()

    loop(GROUP, take_outputs, 1)
    for pair in range(GROUP // 2):
        even, odd = recv_o[2 * pair], recv_o[2 * pair + 1]
        cols = slice(pair * LANES, (pair + 1) * LANES)
        outputs[: DH // 2, cols] = jnp.concatenate([even[:, :DH], odd[:, :DH]], axis=1)
        outputs[DH // 2 :, cols] = jnp.concatenate([even[:, DH:], odd[:, DH:]], axis=1)

    def finish_sends(step):
        w_copy(peer(step), me).wait_send()
        t_copy(peer(step), me).wait_send()
        o_copy(peer(step), me).wait_send()

    loop(GROUP, finish_sends, 1)


def shards(keys, values, rates, queries, gate_up, down_t, step_sizes, gain):
    vmem = pl.BlockSpec(memory_space=pltpu.VMEM)
    smem = pl.BlockSpec(memory_space=pltpu.SMEM)
    bf16, f32 = jnp.bfloat16, jnp.float32
    sems = pltpu.SemaphoreType.DMA((GROUP,))
    return pl.pallas_call(
        whole_kernel,
        out_shape=jax.ShapeDtypeStruct(queries.shape, bf16),
        in_specs=[vmem] * 6 + [smem, vmem],
        out_specs=vmem,
        scratch_shapes=[
            pltpu.VMEM((GROUP, 2 * DH, LANES), bf16),
            pltpu.VMEM((GROUP, 2 * DH, LANES), bf16),
            pltpu.VMEM((GROUP, 2 * DH, LANES), bf16),
            pltpu.VMEM((GROUP // 2, 2 * DH, 2 * LANES), bf16),
            pltpu.VMEM((GROUP, DH // 2, LANES), bf16),
            pltpu.VMEM((GROUP, DH // 2, LANES), bf16),
            pltpu.VMEM((GROUP, LANES), f32),
            pltpu.VMEM((3, HID, DH), bf16),
            pltpu.VMEM((HID, DH), bf16),
            pltpu.VMEM((3, HID, DH), f32),
            pltpu.VMEM((3, HID, DH), bf16),
        ]
        + [sems] * 6
        + [pltpu.SemaphoreType.DMA((3,))],
        compiler_params=pltpu.CompilerParams(
            collective_id=0, has_side_effects=True, vmem_limit_bytes=48 << 20
        ),
    )(keys, values, rates, queries, gate_up, down_t, step_sizes, gain.reshape(GROUP // 2, LANES))


def solution(mesh):
    return jax.shard_map(
        shards,
        mesh=mesh,
        in_specs=(
            P(("scene", "view"), None),
            P(("scene", "view"), None),
            P(("scene", "view"), None),
            P(("scene", "view"), None),
            P(None, None, None, "view"),
            P(None, None, "view"),
            P(),
            P(),
        ),
        out_specs=P(("scene", "view"), None),
        check_vma=False,
    )
```

```python
import jax
import jax.numpy as jnp
from jax import lax
from jax.experimental import pallas as pl
from jax.experimental.pallas import tpu as pltpu
from jax.sharding import PartitionSpec as P

NS_STEPS = 5
GROUP = 16
DH = 64
HID = 1024
LANES = 128

poly_one = 3.4445
poly_two = -4.775
poly_three = 2.0315

ROWS_BY_ROWS = (((1,), (1,)), ((), ()))
COLS_BY_COLS = (((0,), (0,)), ((), ()))


def nt_dot(left, right):
    return lax.dot_general(left, right, ROWS_BY_ROWS, preferred_element_type=jnp.float32)


def plain_dot(left, right):
    return jnp.dot(left, right, preferred_element_type=jnp.float32)


def exact_dot(left, right):
    return jnp.dot(
        left, right, precision=lax.Precision.HIGHEST, preferred_element_type=jnp.float32
    )


def flip(block):
    return block.T


def clear_grads(grad):
    grad[...] = jnp.zeros_like(grad)


def unpack_weights(source, recv_w, weight, query):
    turned = flip(recv_w[source])
    low = pl.ds(pl.multiple_of(source * DH, DH), DH)
    weight[0, low, :] = turned[:DH, :DH]
    weight[1, low, :] = turned[:DH, DH:]
    weight[2, low, :] = turned[DH:, :DH]
    query[low, :] = turned[DH:, DH:]


def grad_chunk(pair, recv_t, weight, grad):
    key_cols = recv_t[pair, :DH, :]
    err_cols = recv_t[pair, DH:, :]

    gate = plain_dot(weight[0], key_cols)
    up = plain_dot(weight[1], key_cols)
    back = plain_dot(weight[2], err_cols)
    sigma = 0.5 * jnp.tanh(0.5 * gate) + 0.5
    gated = gate * sigma
    hidden = (gated * up).astype(jnp.bfloat16)
    up_term = (back * gated).astype(jnp.bfloat16)
    gate_term = (back * up * (sigma + gated * (1.0 - sigma))).astype(jnp.bfloat16)
    grad[0] += nt_dot(gate_term, key_cols)
    grad[1] += nt_dot(up_term, key_cols)
    grad[2] += nt_dot(hidden, err_cols)


def orthogonalizers(grad):
    grams, totals = [], []
    eye = (
        lax.broadcasted_iota(jnp.int32, (DH, DH), 0) == lax.broadcasted_iota(jnp.int32, (DH, DH), 1)
    ).astype(jnp.float32)
    for part in range(3):
        gram = lax.dot_general(
            grad[part],
            grad[part],
            COLS_BY_COLS,
            precision=lax.Precision.HIGHEST,
            preferred_element_type=jnp.float32,
        )
        square_norm = jnp.sum(gram * eye, axis=(0, 1), keepdims=True)
        factor = 1.0 / (jnp.sqrt(square_norm) + 1e-07)
        grams.append(gram * (factor * factor))
        totals.append(factor * eye)
    for step in range(NS_STEPS):
        squares = [exact_dot(gram, gram) for gram in grams]
        blends = [
            poly_one * eye + poly_two * gram + poly_three * square
            for gram, square in zip(grams, squares)
        ]
        totals = [
            blend * total[:1, :1] if step == 0 else exact_dot(blend, total)
            for blend, total in zip(blends, totals)
        ]
        if step < NS_STEPS - 1:
            cubes = [exact_dot(gram, square) for gram, square in zip(grams, squares)]
            halves = [
                poly_one * gram + poly_two * square + poly_three * cube
                for gram, square, cube in zip(grams, squares, cubes)
            ]
            grams = [exact_dot(half, blend) for half, blend in zip(halves, blends)]
    return totals


def renew(grad, weight, fresh, step_size):
    totals = orthogonalizers(grad)
    for part in range(3):
        start = weight[part].astype(jnp.float32)
        moved = start - step_size * exact_dot(grad[part], totals[part])
        keep = jnp.sum(start * start, axis=1, keepdims=True)
        length = jnp.sum(moved * moved, axis=1, keepdims=True)
        fresh[part] = (moved * (jnp.sqrt(keep) / (jnp.sqrt(length) + 1e-06))).astype(jnp.bfloat16)


QROWS = 256


def apply_block(at, query, fresh, gain, send_o):
    rows = pl.ds(pl.multiple_of(at * QROWS, QROWS), QROWS)
    block = query[rows, :]
    hidden = []
    for half in range(4):
        cols = pl.ds(half * 256, 256)
        gate = nt_dot(block, fresh[0, cols, :])
        up = nt_dot(block, fresh[1, cols, :])
        sigma = 0.5 * jnp.tanh(0.5 * gate) + 0.5
        hidden.append((gate * sigma * up).astype(jnp.bfloat16))
    head_out = plain_dot(jnp.concatenate(hidden, axis=1), fresh[2])
    mean_square = jnp.sum(head_out * head_out, axis=1, keepdims=True) * (1.0 / DH)
    done = head_out * lax.rsqrt(mean_square + 1e-06) * gain
    for piece in range(QROWS // DH):
        top = done[piece * DH : piece * DH + DH // 2]
        bottom = done[piece * DH + DH // 2 : (piece + 1) * DH]
        send_o[at * (QROWS // DH) + piece] = jnp.concatenate([top, bottom], axis=1).astype(
            jnp.bfloat16
        )


def turn_tokens(pair, keys, values, rates, send_t):
    cols = pl.ds(pl.multiple_of(pair * LANES, LANES), LANES)
    turned_k = flip(keys[:, cols])
    turned_v = flip(values[:, cols]).astype(jnp.float32)
    pair_rates = rates[...].astype(jnp.float32)
    row = lax.broadcasted_iota(jnp.int32, pair_rates.shape, 0)
    for side in range(2):
        head = 2 * pair + side
        rate = jnp.sum(jnp.where(row == head, pair_rates, 0.0), axis=0, keepdims=True)
        part = slice(side * DH, (side + 1) * DH)
        send_t[head, :DH, :] = turned_k[part]
        send_t[head, DH:, :] = (-(rate * turned_v[part])).astype(jnp.bfloat16)


def pack_weights(pair, queries, gate_up, down_t, send_w):
    cols = pl.ds(pl.multiple_of(pair * LANES, LANES), LANES)
    turned_q = flip(queries[:, cols])
    for side in range(2):
        head = 2 * pair + side
        send_w[head, :DH, :] = jnp.concatenate([gate_up[0, head], down_t[head]], axis=1)
        send_w[head, DH:, :] = jnp.concatenate(
            [gate_up[1, head], turned_q[side * DH : (side + 1) * DH]], axis=1
        )


def whole_kernel(
    keys_hbm,
    values_hbm,
    rates_hbm,
    queries_hbm,
    gate_up_hbm,
    down_t_hbm,
    steps_hbm,
    gain_hbm,
    outputs,
    keys,
    values,
    rates,
    queries,
    gate_up,
    down_t,
    step_sizes,
    gain_rows,
    send_w,
    recv_w,
    send_t,
    recv_t,
    send_o,
    recv_o,
    weight,
    query,
    grad,
    fresh,
    w_out,
    w_in,
    t_out,
    t_in,
    o_out,
    o_in,
    here,
    loaded,
):
    loads = [
        pltpu.make_async_copy(far, near, loaded.at[at])
        for at, (far, near) in enumerate(
            (
                (gate_up_hbm, gate_up),
                (down_t_hbm, down_t),
                (queries_hbm, queries),
                (keys_hbm, keys),
                (values_hbm, values),
                (rates_hbm, rates),
                (steps_hbm, step_sizes),
                (gain_hbm, gain_rows),
            )
        )
    ]
    for load in loads:
        load.start()

    me = lax.axis_index("view")
    my_pair, my_side = me // 2, me % 2
    my_cols = pl.ds(pl.multiple_of(my_side * LANES, LANES), LANES)

    def peer(step):
        return lax.rem(me + step, GROUP)

    def loop(count, one, first=0):
        def loop_body(at, carry):
            one(at)
            return carry

        lax.fori_loop(first, count, loop_body, 0)

    barrier = pltpu.get_barrier_semaphore()

    def greet(step):
        pl.semaphore_signal(
            barrier,
            inc=1,
            device_id={"view": peer(step)},
            device_id_type=pl.DeviceIdType.MESH,
        )

    loop(GROUP, greet, 1)

    def w_copy(target, origin):
        return pltpu.make_async_remote_copy(
            src_ref=send_w.at[target],
            dst_ref=recv_w.at[origin],
            send_sem=w_out.at[target],
            recv_sem=w_in.at[origin],
            device_id={"view": target},
            device_id_type=pl.DeviceIdType.MESH,
        )

    def t_copy(target, origin):
        cols = pl.ds(pl.multiple_of(lax.rem(origin, 2) * LANES, LANES), LANES)
        return pltpu.make_async_remote_copy(
            src_ref=send_t.at[target],
            dst_ref=recv_t.at[lax.div(origin, 2), :, cols],
            send_sem=t_out.at[target],
            recv_sem=t_in.at[origin],
            device_id={"view": target},
            device_id_type=pl.DeviceIdType.MESH,
        )

    def o_copy(target, origin):
        return pltpu.make_async_remote_copy(
            src_ref=send_o.at[target],
            dst_ref=recv_o.at[origin],
            send_sem=o_out.at[target],
            recv_sem=o_in.at[origin],
            device_id={"view": target},
            device_id_type=pl.DeviceIdType.MESH,
        )

    for load in loads[:3]:
        load.wait()
    loop(GROUP // 2, lambda pair: pack_weights(pair, queries, gate_up, down_t, send_w))
    pl.semaphore_wait(barrier, GROUP - 1)

    loop(GROUP, lambda step: w_copy(peer(step), me).start(), 1)
    for load in loads[3:]:
        load.wait()
    loop(GROUP // 2, lambda pair: turn_tokens(pair, keys, values, rates, send_t))
    loop(GROUP, lambda step: t_copy(peer(step), me).start(), 1)

    own_w = pltpu.make_async_copy(send_w.at[me], recv_w.at[me], here.at[0])
    own_t = pltpu.make_async_copy(send_t.at[me], recv_t.at[my_pair, :, my_cols], here.at[1])
    own_w.start()
    own_t.start()
    clear_grads(grad)
    own_w.wait()
    unpack_weights(me, recv_w, weight, query)

    def take_weights(step):
        origin = peer(GROUP - step)
        w_copy(origin, origin).wait_recv()
        unpack_weights(origin, recv_w, weight, query)

    loop(GROUP, take_weights, 1)
    own_t.wait()
    other = my_pair * 2 + 1 - my_side
    t_copy(other, other).wait_recv()
    grad_chunk(my_pair, recv_t, weight, grad)

    def take_tokens(step):
        pair = lax.rem(my_pair + GROUP // 2 - step, GROUP // 2)
        t_copy(2 * pair, 2 * pair).wait_recv()
        t_copy(2 * pair + 1, 2 * pair + 1).wait_recv()
        grad_chunk(pair, recv_t, weight, grad)

    loop(GROUP // 2, take_tokens, 1)

    renew(grad, weight, fresh, step_sizes[me])
    gain = gain_rows[pl.ds(my_pair, 1), :]
    gain = jnp.where(my_side == 0, gain[:, :DH], gain[:, DH:])

    for at in range(HID // QROWS):
        apply_block(at, query, fresh, gain, send_o)
        for target in range(at * (QROWS // DH), (at + 1) * (QROWS // DH)):

            @pl.when(target != me)
            def _():
                o_copy(target, me).start()

    own_o = pltpu.make_async_copy(send_o.at[me], recv_o.at[me], here.at[2])
    own_o.start()
    own_o.wait()

    def take_outputs(step):
        o_copy(peer(step), peer(step)).wait_recv()

    loop(GROUP, take_outputs, 1)
    for pair in range(GROUP // 2):
        even, odd = recv_o[2 * pair], recv_o[2 * pair + 1]
        cols = slice(pair * LANES, (pair + 1) * LANES)
        outputs[: DH // 2, cols] = jnp.concatenate([even[:, :DH], odd[:, :DH]], axis=1)
        outputs[DH // 2 :, cols] = jnp.concatenate([even[:, DH:], odd[:, DH:]], axis=1)

    def finish_sends(step):
        w_copy(peer(step), me).wait_send()
        t_copy(peer(step), me).wait_send()
        o_copy(peer(step), me).wait_send()

    loop(GROUP, finish_sends, 1)


def shards(keys, values, rates, queries, gate_up, down_t, step_sizes, gain):
    bf16, f32 = jnp.bfloat16, jnp.float32
    sems = pltpu.SemaphoreType.DMA((GROUP,))
    return pl.pallas_call(
        whole_kernel,
        out_shape=jax.ShapeDtypeStruct(queries.shape, bf16),
        in_specs=[pl.BlockSpec(memory_space=pltpu.HBM)] * 8,
        out_specs=pl.BlockSpec(memory_space=pltpu.VMEM),
        scratch_shapes=[
            pltpu.VMEM(keys.shape, bf16),
            pltpu.VMEM(values.shape, bf16),
            pltpu.VMEM(rates.shape[::-1], bf16),
            pltpu.VMEM(queries.shape, bf16),
            pltpu.VMEM(gate_up.shape, bf16),
            pltpu.VMEM(down_t.shape, bf16),
            pltpu.SMEM(step_sizes.shape, f32),
            pltpu.VMEM((GROUP // 2, LANES), f32),
            pltpu.VMEM((GROUP, 2 * DH, LANES), bf16),
            pltpu.VMEM((GROUP, 2 * DH, LANES), bf16),
            pltpu.VMEM((GROUP, 2 * DH, LANES), bf16),
            pltpu.VMEM((GROUP // 2, 2 * DH, 2 * LANES), bf16),
            pltpu.VMEM((GROUP, DH // 2, LANES), bf16),
            pltpu.VMEM((GROUP, DH // 2, LANES), bf16),
            pltpu.VMEM((3, HID, DH), bf16),
            pltpu.VMEM((HID, DH), bf16),
            pltpu.VMEM((3, HID, DH), f32),
            pltpu.VMEM((3, HID, DH), bf16),
        ]
        + [sems] * 6
        + [pltpu.SemaphoreType.DMA((3,)), pltpu.SemaphoreType.DMA((8,))],
        compiler_params=pltpu.CompilerParams(
            collective_id=0, has_side_effects=True, vmem_limit_bytes=48 << 20
        ),
    )(
        keys,
        values,
        rates.T,
        queries,
        gate_up,
        down_t,
        step_sizes,
        gain.reshape(GROUP // 2, LANES),
    )


def solution(mesh):
    return jax.shard_map(
        shards,
        mesh=mesh,
        in_specs=(
            P(("scene", "view"), None),
            P(("scene", "view"), None),
            P(("scene", "view"), None),
            P(("scene", "view"), None),
            P(None, None, None, "view"),
            P(None, None, "view"),
            P(),
            P(),
        ),
        out_specs=P(("scene", "view"), None),
        check_vma=False,
    )
```

```python
import jax
import jax.numpy as jnp
from jax import lax
from jax.experimental import pallas as pl
from jax.experimental.pallas import tpu as pltpu
from jax.sharding import PartitionSpec as P

NS_STEPS = 5
GROUP = 16
PAIRS = GROUP // 2
DH = 64
HID = 1024
LANES = 128
COLS = 256

poly_one = 3.4445
poly_two = -4.775
poly_three = 2.0315

ROWS_BY_ROWS = (((1,), (1,)), ((), ()))
COLS_BY_COLS = (((0,), (0,)), ((), ()))


def plain_dot(left, right):
    return jnp.dot(left, right, preferred_element_type=jnp.float32)


def nt_dot(left, right):
    return lax.dot_general(left, right, ROWS_BY_ROWS, preferred_element_type=jnp.float32)


def exact_dot(left, right):
    return jnp.dot(
        left, right, precision=lax.Precision.HIGHEST, preferred_element_type=jnp.float32
    )


def side_by_side(left, right):
    return jnp.concatenate([left, right], axis=1)


def clear_grads(grad):
    grad[...] = jnp.zeros_like(grad)


def unpack_weights(pair, recv_w, weight):
    even, odd = recv_w[2 * pair], recv_w[2 * pair + 1]
    cols = pl.ds(pl.multiple_of(pair * LANES, LANES), LANES)
    weight[0, :, cols] = side_by_side(even[:DH, :DH], odd[:DH, :DH])
    weight[1, :, cols] = side_by_side(even[:DH, DH:], odd[:DH, DH:])
    weight[2, : DH // 2, cols] = side_by_side(even[DH:, :DH], odd[DH:, :DH])
    weight[2, DH // 2 :, cols] = side_by_side(even[DH:, DH:], odd[DH:, DH:])


def make_terms(slot, cols, keys, errors, weight, terms):
    gate = plain_dot(keys, weight[0, :, cols])
    up = plain_dot(keys, weight[1, :, cols])
    back = plain_dot(errors, weight[2, :, cols])
    sigma = 0.5 * jnp.tanh(0.5 * gate) + 0.5
    gated = gate * sigma
    terms[slot, 0, :, cols] = (back * up * (sigma + gated * (1.0 - sigma))).astype(jnp.bfloat16)
    terms[slot, 1, :, cols] = (back * gated).astype(jnp.bfloat16)
    terms[slot, 2, :, cols] = (gated * up).astype(jnp.bfloat16)


def add_grads(slot, cols, turned, terms, grad):
    grad[0, :, cols] += plain_dot(turned[slot, :DH, :], terms[slot, 0, :, cols])
    grad[1, :, cols] += plain_dot(turned[slot, :DH, :], terms[slot, 1, :, cols])
    grad[2, :, cols] += plain_dot(turned[slot, DH:, :], terms[slot, 2, :, cols])


def grad_chunk(pair, slot, recv_t, weight, turned, terms, grad, fill=True, drain=True):
    if fill:
        block = recv_t[pl.ds(2 * pair, 2)].reshape(2 * LANES, LANES)
        turned[slot] = block.T
        keys, errors = block[:, :DH], block[:, DH:]
    for at in range(HID // COLS):
        cols = slice(at * COLS, (at + 1) * COLS)
        if fill:
            make_terms(slot, cols, keys, errors, weight, terms)
        if drain:
            add_grads(1 - slot, cols, turned, terms, grad)


def split_three(value):
    high = value.astype(jnp.bfloat16)
    rest = value - high.astype(jnp.float32)
    middle = rest.astype(jnp.bfloat16)
    low = (rest - middle.astype(jnp.float32)).astype(jnp.bfloat16)
    return high, middle, low


def orthogonalizers(pieces):
    grams, totals = [], []
    eye = (
        lax.broadcasted_iota(jnp.int32, (DH, DH), 0) == lax.broadcasted_iota(jnp.int32, (DH, DH), 1)
    ).astype(jnp.float32)
    for part in pieces:
        stacked = jnp.concatenate(part, axis=0)
        blocks = nt_dot(stacked, stacked)
        gram = sum(
            blocks[a * DH : (a + 1) * DH, b * DH : (b + 1) * DH]
            for a, b in ((1, 1), (0, 2), (2, 0), (0, 1), (1, 0), (0, 0))
        )
        square_norm = jnp.sum(gram * eye, axis=(0, 1), keepdims=True)
        factor = 1.0 / (jnp.sqrt(square_norm) + 1e-07)
        grams.append(gram * (factor * factor))
        totals.append(factor)
    for step in range(NS_STEPS):
        squares = [exact_dot(gram, gram) for gram in grams]
        blends = [
            poly_one * eye + poly_two * gram + poly_three * square
            for gram, square in zip(grams, squares)
        ]
        totals = [
            blend * total if step == 0 else exact_dot(blend, total)
            for blend, total in zip(blends, totals)
        ]
        if step < NS_STEPS - 1:
            cubes = [exact_dot(gram, square) for gram, square in zip(grams, squares)]
            halves = [
                poly_one * gram + poly_two * square + poly_three * cube
                for gram, square, cube in zip(grams, squares, cubes)
            ]
            grams = [exact_dot(half, blend) for half, blend in zip(halves, blends)]
    return totals


def renew(grad, weight, fresh, turned_down, step_size):
    pieces = [split_three(grad[part]) for part in range(3)]
    totals = orthogonalizers(pieces)
    for part in range(3):
        high, middle, _ = split_three(totals[part])
        left = jnp.concatenate([high, high, middle, middle], axis=1)
        right = jnp.concatenate([pieces[part][0], pieces[part][1]] * 2, axis=0)
        start = weight[part].astype(jnp.float32)
        moved = start - step_size * plain_dot(left, right)
        keep = jnp.sum(start * start, axis=0, keepdims=True)
        length = jnp.sum(moved * moved, axis=0, keepdims=True)
        moved = (moved * (jnp.sqrt(keep) / (jnp.sqrt(length) + 1e-06))).astype(jnp.bfloat16)
        if part < 2:
            fresh[part] = moved
        else:
            turned_down[...] = moved.T


SOURCES = 4


def apply_block(at, recv_q, fresh, turned_down, gain, send_o):
    take = pl.ds(at * SOURCES, SOURCES)
    count = SOURCES * DH // 2
    block = jnp.concatenate(
        [recv_q[take, :, :DH].reshape(count, DH), recv_q[take, :, DH:].reshape(count, DH)], axis=0
    )
    hidden = []
    for part in range(HID // COLS):
        cols = slice(part * COLS, (part + 1) * COLS)
        gate = plain_dot(block, fresh[0, :, cols])
        up = plain_dot(block, fresh[1, :, cols])
        sigma = 0.5 * jnp.tanh(0.5 * gate) + 0.5
        hidden.append((gate * sigma * up).astype(jnp.bfloat16))
    head_out = plain_dot(jnp.concatenate(hidden, axis=1), turned_down[...])
    mean_square = jnp.sum(head_out * head_out, axis=1, keepdims=True) * (1.0 / DH)
    done = head_out * lax.rsqrt(mean_square + 1e-06) * gain
    packed = side_by_side(done[:count], done[count:]).astype(jnp.bfloat16)
    send_o[take] = packed.reshape(SOURCES, DH // 2, LANES)


def pack_tokens(keys, values, rates, send_t):
    head_of = lax.broadcasted_iota(jnp.int32, (GROUP, LANES), 1) // DH
    row = lax.broadcasted_iota(jnp.int32, (GROUP, LANES), 0)
    for pair in range(PAIRS):
        cols = slice(pair * LANES, (pair + 1) * LANES)
        spread = (row == head_of + 2 * pair).astype(jnp.bfloat16)
        rate = lax.dot_general(
            rates[...], spread, COLS_BY_COLS, preferred_element_type=jnp.float32
        )
        error = (-(rate * values[:, cols].astype(jnp.float32))).astype(jnp.bfloat16)
        key = keys[:, cols]
        send_t[2 * pair] = side_by_side(key[:, :DH], error[:, :DH])
        send_t[2 * pair + 1] = side_by_side(key[:, DH:], error[:, DH:])


def pack_queries(queries, send_q):
    half = DH // 2
    for pair in range(PAIRS):
        cols = slice(pair * LANES, (pair + 1) * LANES)
        top, bottom = queries[:half, cols], queries[half:, cols]
        send_q[2 * pair] = side_by_side(top[:, :DH], bottom[:, :DH])
        send_q[2 * pair + 1] = side_by_side(top[:, DH:], bottom[:, DH:])


def pack_weights(gate_up, down_t, send_w):
    for head in range(GROUP):
        send_w[head, :DH, :] = side_by_side(gate_up[0, head], gate_up[1, head])
        down = down_t[head]
        send_w[head, DH:, :] = side_by_side(down[: DH // 2], down[DH // 2 :])


def whole_kernel(
    keys_hbm,
    values_hbm,
    rates_hbm,
    queries_hbm,
    gate_up_hbm,
    down_t_hbm,
    steps_hbm,
    gain_hbm,
    outputs,
    keys,
    values,
    rates,
    queries,
    gate_up,
    down_t,
    step_sizes,
    gain_rows,
    send_w,
    recv_w,
    send_t,
    recv_t,
    send_q,
    recv_q,
    send_o,
    recv_o,
    weight,
    turned,
    terms,
    grad,
    fresh,
    turned_down,
    out_sems,
    in_sems,
    here,
    loaded,
):
    me = lax.axis_index("view")
    my_pair, my_side = me // 2, me % 2

    def peer(step):
        return lax.rem(me + step, GROUP)

    def loop(first, count, one):
        def loop_body(at, carry):
            one(at)
            return carry

        lax.fori_loop(first, count, loop_body, 0)

    loads = [
        pltpu.make_async_copy(far, near, loaded.at[at])
        for at, (far, near) in enumerate(
            (
                (gate_up_hbm, gate_up),
                (down_t_hbm, down_t),
                (keys_hbm, keys),
                (values_hbm, values),
                (rates_hbm, rates),
                (queries_hbm, queries),
                (steps_hbm, step_sizes),
                (gain_hbm, gain_rows),
            )
        )
    ]
    for load in loads:
        load.start()

    barrier = pltpu.get_barrier_semaphore()

    def greet(step):
        pl.semaphore_signal(
            barrier,
            inc=1,
            device_id={"view": peer(step)},
            device_id_type=pl.DeviceIdType.MESH,
        )

    loop(1, GROUP, greet)

    def copy(kind, source, target_buffer):
        def build(target, origin):
            return pltpu.make_async_remote_copy(
                src_ref=source.at[target],
                dst_ref=target_buffer.at[origin],
                send_sem=out_sems.at[kind, target],
                recv_sem=in_sems.at[kind, origin],
                device_id={"view": target},
                device_id_type=pl.DeviceIdType.MESH,
            )

        return build

    w_copy = copy(0, send_w, recv_w)
    t_copy = copy(1, send_t, recv_t)
    q_copy = copy(2, send_q, recv_q)
    o_copy = copy(3, send_o, recv_o)

    for load in loads[:2]:
        load.wait()
    pack_weights(gate_up, down_t, send_w)
    pl.semaphore_wait(barrier, GROUP - 1)
    loop(1, GROUP, lambda step: w_copy(peer(step), me).start())
    for load in loads[2:5]:
        load.wait()
    pack_tokens(keys, values, rates, send_t)
    loop(1, GROUP, lambda step: t_copy(peer(step), me).start())
    for load in loads[5:]:
        load.wait()
    pack_queries(queries, send_q)
    loop(1, GROUP, lambda step: q_copy(peer(step), me).start())

    own = [
        pltpu.make_async_copy(source.at[me], target.at[me], here.at[at])
        for at, (source, target) in enumerate(
            ((send_w, recv_w), (send_t, recv_t), (send_q, recv_q))
        )
    ]
    for copied in own:
        copied.start()
    clear_grads(grad)
    for copied in own:
        copied.wait()

    loop(1, GROUP, lambda step: w_copy(peer(step), peer(step)).wait_recv())
    for pair in range(PAIRS):
        unpack_weights(pair, recv_w, weight)

    def pair_at(step):
        return lax.rem(my_pair + PAIRS - step, PAIRS)

    def take_tokens(step):
        pair = pair_at(step)
        t_copy(2 * pair, 2 * pair).wait_recv()
        t_copy(2 * pair + 1, 2 * pair + 1).wait_recv()
        return pair

    other = my_pair * 2 + 1 - my_side
    t_copy(other, other).wait_recv()
    grad_chunk(my_pair, 0, recv_t, weight, turned, terms, grad, drain=False)

    def two_chunks(at):
        for side in range(2):
            pair = take_tokens(2 * at + 1 + side)
            grad_chunk(pair, 1 - side, recv_t, weight, turned, terms, grad)

    loop(0, PAIRS // 2 - 1, two_chunks)
    grad_chunk(take_tokens(PAIRS - 1), 1, recv_t, weight, turned, terms, grad)
    grad_chunk(0, 0, recv_t, weight, turned, terms, grad, fill=False)

    renew(grad, weight, fresh, turned_down, step_sizes[me])
    gain = gain_rows[pl.ds(my_pair, 1), :]
    gain = jnp.where(my_side == 0, gain[:, :DH], gain[:, DH:])
    loop(1, GROUP, lambda step: q_copy(peer(step), peer(step)).wait_recv())

    for at in range(GROUP // SOURCES):
        apply_block(at, recv_q, fresh, turned_down, gain, send_o)
        for target in range(at * SOURCES, (at + 1) * SOURCES):

            @pl.when(target != me)
            def _():
                o_copy(target, me).start()

    own_o = pltpu.make_async_copy(send_o.at[me], recv_o.at[me], here.at[3])
    own_o.start()
    own_o.wait()
    loop(1, GROUP, lambda step: o_copy(peer(step), peer(step)).wait_recv())
    half = DH // 2
    for pair in range(PAIRS):
        even, odd = recv_o[2 * pair], recv_o[2 * pair + 1]
        cols = slice(pair * LANES, (pair + 1) * LANES)
        outputs[:half, cols] = side_by_side(even[:, :DH], odd[:, :DH])
        outputs[half:, cols] = side_by_side(even[:, DH:], odd[:, DH:])

    def finish_sends(step):
        for build in (w_copy, t_copy, q_copy, o_copy):
            build(peer(step), me).wait_send()

    loop(1, GROUP, finish_sends)


def shards(keys, values, rates, queries, gate_up, down_t, step_sizes, gain):
    bf16, f32 = jnp.bfloat16, jnp.float32

    def boxes(rows):
        return [pltpu.VMEM((GROUP, rows, LANES), bf16)] * 2

    return pl.pallas_call(
        whole_kernel,
        out_shape=jax.ShapeDtypeStruct(queries.shape, bf16),
        in_specs=[pl.BlockSpec(memory_space=pltpu.HBM)] * 8,
        out_specs=pl.BlockSpec(memory_space=pltpu.VMEM),
        scratch_shapes=[
            pltpu.VMEM(keys.shape, bf16),
            pltpu.VMEM(values.shape, bf16),
            pltpu.VMEM(rates.shape[::-1], bf16),
            pltpu.VMEM(queries.shape, bf16),
            pltpu.VMEM(gate_up.shape, bf16),
            pltpu.VMEM(down_t.shape, bf16),
            pltpu.SMEM(step_sizes.shape, f32),
            pltpu.VMEM((PAIRS, LANES), f32),
        ]
        + boxes(DH + DH // 2)
        + boxes(LANES)
        + boxes(DH // 2)
        + boxes(DH // 2)
        + [
            pltpu.VMEM((3, DH, HID), bf16),
            pltpu.VMEM((2, 2 * DH, 2 * LANES), bf16),
            pltpu.VMEM((2, 3, 2 * LANES, HID), bf16),
            pltpu.VMEM((3, DH, HID), f32),
            pltpu.VMEM((2, DH, HID), bf16),
            pltpu.VMEM((HID, DH), bf16),
            pltpu.SemaphoreType.DMA((4, GROUP)),
            pltpu.SemaphoreType.DMA((4, GROUP)),
            pltpu.SemaphoreType.DMA((4,)),
            pltpu.SemaphoreType.DMA((8,)),
        ],
        compiler_params=pltpu.CompilerParams(
            collective_id=0, has_side_effects=True, vmem_limit_bytes=60 << 20
        ),
    )(
        keys,
        values,
        rates.T,
        queries,
        gate_up,
        down_t,
        step_sizes,
        gain.reshape(PAIRS, LANES),
    )


def solution(mesh):
    return jax.shard_map(
        shards,
        mesh=mesh,
        in_specs=(
            P(("scene", "view"), None),
            P(("scene", "view"), None),
            P(("scene", "view"), None),
            P(("scene", "view"), None),
            P(None, None, None, "view"),
            P(None, None, "view"),
            P(),
            P(),
        ),
        out_specs=P(("scene", "view"), None),
        check_vma=False,
    )
```

```python
import jax
import jax.numpy as jnp
from jax import lax
from jax.experimental import pallas as pl
from jax.experimental.pallas import tpu as pltpu
from jax.sharding import PartitionSpec as P

NS_STEPS = 5
GROUP = 16
PAIRS = GROUP // 2
DH = 64
HID = 1024
LANES = 128
COLS = 256

poly_one = 3.4445
poly_two = -4.775
poly_three = 2.0315

ROWS_BY_ROWS = (((1,), (1,)), ((), ()))
COLS_BY_COLS = (((0,), (0,)), ((), ()))


def plain_dot(left, right):
    return jnp.dot(left, right, preferred_element_type=jnp.float32)


def nt_dot(left, right):
    return lax.dot_general(left, right, ROWS_BY_ROWS, preferred_element_type=jnp.float32)


def side_by_side(left, right):
    return jnp.concatenate([left, right], axis=1)


def clear_grads(grad):
    grad[...] = jnp.zeros_like(grad)


def unpack_weights(pair, recv_w, weight):
    even, odd = recv_w[2 * pair], recv_w[2 * pair + 1]
    cols = pl.ds(pl.multiple_of(pair * LANES, LANES), LANES)
    weight[0, :, cols] = side_by_side(even[:DH, :DH], odd[:DH, :DH])
    weight[1, :, cols] = side_by_side(even[:DH, DH:], odd[:DH, DH:])
    weight[2, : DH // 2, cols] = side_by_side(even[DH:, :DH], odd[DH:, :DH])
    weight[2, DH // 2 :, cols] = side_by_side(even[DH:, DH:], odd[DH:, DH:])


def make_terms(slot, cols, keys, errors, weight, terms):
    gate = plain_dot(keys, weight[0, :, cols])
    up = plain_dot(keys, weight[1, :, cols])
    back = plain_dot(errors, weight[2, :, cols])
    sigma = 0.5 * jnp.tanh(0.5 * gate) + 0.5
    gated = gate * sigma
    terms[slot, 0, :, cols] = (back * up * (sigma + gated * (1.0 - sigma))).astype(jnp.bfloat16)
    terms[slot, 1, :, cols] = (back * gated).astype(jnp.bfloat16)
    terms[slot, 2, :, cols] = (gated * up).astype(jnp.bfloat16)


def add_grads(slot, cols, turned, terms, grad):
    grad[0, :, cols] += plain_dot(turned[slot, :DH, :], terms[slot, 0, :, cols])
    grad[1, :, cols] += plain_dot(turned[slot, :DH, :], terms[slot, 1, :, cols])
    grad[2, :, cols] += plain_dot(turned[slot, DH:, :], terms[slot, 2, :, cols])


def grad_chunk(pair, slot, recv_t, weight, turned, terms, grad, fill=True, drain=True):
    if fill:
        block = recv_t[pl.ds(2 * pair, 2)].reshape(2 * LANES, LANES)
        turned[slot] = block.T
        keys, errors = block[:, :DH], block[:, DH:]
    for at in range(HID // COLS):
        cols = slice(at * COLS, (at + 1) * COLS)
        if fill:
            make_terms(slot, cols, keys, errors, weight, terms)
        if drain:
            add_grads(1 - slot, cols, turned, terms, grad)


def split_three(value):
    high = value.astype(jnp.bfloat16)
    rest = value - high.astype(jnp.float32)
    middle = rest.astype(jnp.bfloat16)
    low = (rest - middle.astype(jnp.float32)).astype(jnp.bfloat16)
    return high, middle, low


def twin(value):
    return side_by_side(value, value)


def first_half(shape):
    return lax.broadcasted_iota(jnp.int32, shape, 1) < DH


def exact_twins(left, right):
    high, middle, low = left
    near = first_half(high.shape)
    wide = jnp.concatenate(
        [high, jnp.where(near, middle, high), jnp.where(near, middle, low)], axis=1
    )
    high, middle, low = right
    tall = jnp.concatenate([high, middle, high, low, middle, high], axis=0)
    return plain_dot(wide, tall)


def start_gram(part):
    high, middle, low = part
    stacked = jnp.concatenate([high, middle, low], axis=0)
    blocks = nt_dot(stacked, stacked)
    main = blocks[:DH, :LANES] + blocks[DH : 2 * DH, :LANES]
    side = blocks[2 * DH :, :DH] + blocks[:DH, 2 * DH :]
    return twin(main[:, :DH] + (main[:, DH:] + side))


def orthogonalizers(pieces):
    shape = (DH, 2 * DH)
    row = lax.broadcasted_iota(jnp.int32, shape, 0)
    eye = (row == lax.broadcasted_iota(jnp.int32, shape, 1) % DH).astype(jnp.float32)
    grams, totals = [], []
    for part in pieces:
        gram = start_gram(part)
        square_norm = 0.5 * jnp.sum(gram * eye, axis=(0, 1), keepdims=True)
        factor = 1.0 / (jnp.sqrt(square_norm) + 1e-07)
        grams.append(gram * (factor * factor))
        totals.append(factor)
    for step in range(NS_STEPS):
        cut = [split_three(gram) for gram in grams]
        squares = [exact_twins(one, one) for one in cut]
        blends = [
            poly_one * eye + poly_two * gram + poly_three * square
            for gram, square in zip(grams, squares)
        ]
        cut_blends = [split_three(blend) for blend in blends]
        if step < NS_STEPS - 1:
            cubes = [exact_twins(one, split_three(square)) for one, square in zip(cut, squares)]
            halves = [
                poly_one * gram + poly_two * square + poly_three * cube
                for gram, square, cube in zip(grams, squares, cubes)
            ]
            grams = [
                exact_twins(split_three(half), blend) for half, blend in zip(halves, cut_blends)
            ]
        totals = [
            blend * total if step == 0 else exact_twins(cut_blend, split_three(total))
            for blend, cut_blend, total in zip(blends, cut_blends, totals)
        ]
    return totals


def renew(grad, weight, fresh, turned_down, step_size):
    pieces = [split_three(grad[part]) for part in range(3)]
    totals = orthogonalizers(pieces)
    for part in range(3):
        high, middle, _ = split_three(totals[part])
        right = jnp.concatenate([pieces[part][0], pieces[part][1]] * 2, axis=0)
        start = weight[part].astype(jnp.float32)
        moved = start - step_size * plain_dot(side_by_side(high, middle), right)
        keep = jnp.sum(start * start, axis=0, keepdims=True)
        length = jnp.sum(moved * moved, axis=0, keepdims=True)
        moved = (moved * (jnp.sqrt(keep) / (jnp.sqrt(length) + 1e-06))).astype(jnp.bfloat16)
        if part < 2:
            fresh[part] = moved
        else:
            turned_down[...] = moved.T


SOURCES = 4


def apply_block(at, recv_q, fresh, turned_down, gain, send_o):
    take = pl.ds(at * SOURCES, SOURCES)
    count = SOURCES * DH // 2
    block = jnp.concatenate(
        [recv_q[take, :, :DH].reshape(count, DH), recv_q[take, :, DH:].reshape(count, DH)], axis=0
    )
    hidden = []
    for part in range(HID // COLS):
        cols = slice(part * COLS, (part + 1) * COLS)
        gate = plain_dot(block, fresh[0, :, cols])
        up = plain_dot(block, fresh[1, :, cols])
        sigma = 0.5 * jnp.tanh(0.5 * gate) + 0.5
        hidden.append((gate * sigma * up).astype(jnp.bfloat16))
    head_out = plain_dot(jnp.concatenate(hidden, axis=1), turned_down[...])
    mean_square = jnp.sum(head_out * head_out, axis=1, keepdims=True) * (1.0 / DH)
    done = head_out * lax.rsqrt(mean_square + 1e-06) * gain
    packed = side_by_side(done[:count], done[count:]).astype(jnp.bfloat16)
    send_o[take] = packed.reshape(SOURCES, DH // 2, LANES)


def pack_tokens(keys, values, rates, send_t):
    head_of = lax.broadcasted_iota(jnp.int32, (GROUP, LANES), 1) // DH
    row = lax.broadcasted_iota(jnp.int32, (GROUP, LANES), 0)
    for pair in range(PAIRS):
        cols = slice(pair * LANES, (pair + 1) * LANES)
        spread = (row == head_of + 2 * pair).astype(jnp.bfloat16)
        rate = lax.dot_general(
            rates[...], spread, COLS_BY_COLS, preferred_element_type=jnp.float32
        )
        error = (-(rate * values[:, cols].astype(jnp.float32))).astype(jnp.bfloat16)
        key = keys[:, cols]
        send_t[2 * pair] = side_by_side(key[:, :DH], error[:, :DH])
        send_t[2 * pair + 1] = side_by_side(key[:, DH:], error[:, DH:])


def pack_queries(queries, send_q):
    half = DH // 2
    for pair in range(PAIRS):
        cols = slice(pair * LANES, (pair + 1) * LANES)
        top, bottom = queries[:half, cols], queries[half:, cols]
        send_q[2 * pair] = side_by_side(top[:, :DH], bottom[:, :DH])
        send_q[2 * pair + 1] = side_by_side(top[:, DH:], bottom[:, DH:])


def pack_weights(gate_up, down_t, send_w):
    for head in range(GROUP):
        send_w[head, :DH, :] = side_by_side(gate_up[0, head], gate_up[1, head])
        down = down_t[head]
        send_w[head, DH:, :] = side_by_side(down[: DH // 2], down[DH // 2 :])


def whole_kernel(
    keys_hbm,
    values_hbm,
    rates_hbm,
    queries_hbm,
    gate_up_hbm,
    down_t_hbm,
    steps_hbm,
    gain_hbm,
    outputs,
    keys,
    values,
    rates,
    queries,
    gate_up,
    down_t,
    step_sizes,
    gain_rows,
    send_w,
    recv_w,
    send_t,
    recv_t,
    send_q,
    recv_q,
    send_o,
    recv_o,
    weight,
    turned,
    terms,
    grad,
    fresh,
    turned_down,
    out_sems,
    in_sems,
    here,
    loaded,
):
    me = lax.axis_index("view")
    my_pair, my_side = me // 2, me % 2
    my_row, my_depth = me // 4, my_pair % 2
    partner = 2 * my_pair + 1 - my_side

    def peer(step):
        return lax.rem(me + step, GROUP)

    def chip(rows, depth):
        return ((my_row + rows) % 4) * 2 + (my_depth + depth) % 2

    def loop(first, count, one):
        def loop_body(at, carry):
            one(at)
            return carry

        lax.fori_loop(first, count, loop_body, 0)

    loads = [
        pltpu.make_async_copy(far, near, loaded.at[at])
        for at, (far, near) in enumerate(
            (
                (gate_up_hbm, gate_up),
                (down_t_hbm, down_t),
                (keys_hbm, keys),
                (values_hbm, values),
                (rates_hbm, rates),
                (queries_hbm, queries),
                (steps_hbm, step_sizes),
                (gain_hbm, gain_rows),
            )
        )
    ]
    for load in loads:
        load.start()

    barrier = pltpu.get_barrier_semaphore()

    def greet(target):
        pl.semaphore_signal(
            barrier, inc=1, device_id={"view": target}, device_id_type=pl.DeviceIdType.MESH
        )

    for rows in (2, 1, 3, 0):
        for depth in (1, 0):
            if rows or depth:
                greet(2 * chip(rows, depth))
                greet(2 * chip(rows, depth) + 1)
    greet(partner)

    def to_all(build):
        build(partner, me).start()

        def send(step):
            there = PAIRS - step
            pair = chip(4 - there // 2, there % 2)
            build(2 * pair, me).start()
            build(2 * pair + 1, me).start()

        loop(1, PAIRS, send)

    def copy(kind, source, target_buffer):
        def build(target, origin):
            return pltpu.make_async_remote_copy(
                src_ref=source.at[target],
                dst_ref=target_buffer.at[origin],
                send_sem=out_sems.at[kind, target],
                recv_sem=in_sems.at[kind, origin],
                device_id={"view": target},
                device_id_type=pl.DeviceIdType.MESH,
            )

        return build

    w_copy = copy(0, send_w, recv_w)
    t_copy = copy(1, send_t, recv_t)
    q_copy = copy(2, send_q, recv_q)
    o_copy = copy(3, send_o, recv_o)

    for load in loads[:2]:
        load.wait()
    pack_weights(gate_up, down_t, send_w)
    pl.semaphore_wait(barrier, GROUP - 1)
    to_all(w_copy)
    for load in loads[2:5]:
        load.wait()
    pack_tokens(keys, values, rates, send_t)
    to_all(t_copy)
    for load in loads[5:]:
        load.wait()
    pack_queries(queries, send_q)
    to_all(q_copy)

    own = [
        pltpu.make_async_copy(source.at[me], target.at[me], here.at[at])
        for at, (source, target) in enumerate(
            ((send_w, recv_w), (send_t, recv_t), (send_q, recv_q))
        )
    ]
    for copied in own:
        copied.start()
    clear_grads(grad)
    for copied in own:
        copied.wait()

    loop(1, GROUP, lambda step: w_copy(peer(step), peer(step)).wait_recv())
    for pair in range(PAIRS):
        unpack_weights(pair, recv_w, weight)

    def take_tokens(step):
        there = PAIRS - step
        pair = chip(there // 2, there % 2)
        t_copy(2 * pair, 2 * pair).wait_recv()
        t_copy(2 * pair + 1, 2 * pair + 1).wait_recv()
        return pair

    t_copy(partner, partner).wait_recv()
    grad_chunk(my_pair, 0, recv_t, weight, turned, terms, grad, drain=False)

    def two_chunks(at):
        for side in range(2):
            pair = take_tokens(2 * at + 1 + side)
            grad_chunk(pair, 1 - side, recv_t, weight, turned, terms, grad)

    loop(0, PAIRS // 2 - 1, two_chunks)
    grad_chunk(take_tokens(PAIRS - 1), 1, recv_t, weight, turned, terms, grad)
    grad_chunk(0, 0, recv_t, weight, turned, terms, grad, fill=False)

    renew(grad, weight, fresh, turned_down, step_sizes[me])
    gain = gain_rows[pl.ds(my_pair, 1), :]
    gain = jnp.where(my_side == 0, gain[:, :DH], gain[:, DH:])
    loop(1, GROUP, lambda step: q_copy(peer(step), peer(step)).wait_recv())

    for rows in (2, 1, 3, 0):
        block = (my_row + rows) % 4
        apply_block(block, recv_q, fresh, turned_down, gain, send_o)
        for depth in (1, 0):
            pair = chip(rows, depth)
            if rows or depth:
                o_copy(2 * pair, me).start()
                o_copy(2 * pair + 1, me).start()
    o_copy(partner, me).start()
    own_o = pltpu.make_async_copy(send_o.at[me], recv_o.at[me], here.at[3])
    own_o.start()

    def finish_sends(step):
        for build in (w_copy, t_copy, q_copy, o_copy):
            build(peer(step), me).wait_send()

    loop(1, GROUP, finish_sends)
    own_o.wait()
    loop(1, GROUP, lambda step: o_copy(peer(step), peer(step)).wait_recv())
    half = DH // 2
    for pair in range(PAIRS):
        even, odd = recv_o[2 * pair], recv_o[2 * pair + 1]
        cols = slice(pair * LANES, (pair + 1) * LANES)
        outputs[:half, cols] = side_by_side(even[:, :DH], odd[:, :DH])
        outputs[half:, cols] = side_by_side(even[:, DH:], odd[:, DH:])


def shards(keys, values, rates, queries, gate_up, down_t, step_sizes, gain):
    bf16, f32 = jnp.bfloat16, jnp.float32

    def boxes(rows):
        return [pltpu.VMEM((GROUP, rows, LANES), bf16)] * 2

    return pl.pallas_call(
        whole_kernel,
        out_shape=pltpu.VMEM(queries.shape, bf16),
        in_specs=[pl.BlockSpec(memory_space=pltpu.HBM)] * 8,
        out_specs=pl.BlockSpec(memory_space=pltpu.VMEM),
        scratch_shapes=[
            pltpu.VMEM(keys.shape, bf16),
            pltpu.VMEM(values.shape, bf16),
            pltpu.VMEM(rates.shape[::-1], bf16),
            pltpu.VMEM(queries.shape, bf16),
            pltpu.VMEM(gate_up.shape, bf16),
            pltpu.VMEM(down_t.shape, bf16),
            pltpu.SMEM(step_sizes.shape, f32),
            pltpu.VMEM((PAIRS, LANES), f32),
        ]
        + boxes(DH + DH // 2)
        + boxes(LANES)
        + boxes(DH // 2)
        + boxes(DH // 2)
        + [
            pltpu.VMEM((3, DH, HID), bf16),
            pltpu.VMEM((2, 2 * DH, 2 * LANES), bf16),
            pltpu.VMEM((2, 3, 2 * LANES, HID), bf16),
            pltpu.VMEM((3, DH, HID), f32),
            pltpu.VMEM((2, DH, HID), bf16),
            pltpu.VMEM((HID, DH), bf16),
            pltpu.SemaphoreType.DMA((4, GROUP)),
            pltpu.SemaphoreType.DMA((4, GROUP)),
            pltpu.SemaphoreType.DMA((4,)),
            pltpu.SemaphoreType.DMA((8,)),
        ],
        compiler_params=pltpu.CompilerParams(
            collective_id=0, has_side_effects=True, vmem_limit_bytes=60 << 20
        ),
    )(
        keys,
        values,
        rates.T,
        queries,
        gate_up,
        down_t,
        step_sizes,
        gain.reshape(PAIRS, LANES),
    )


def solution(mesh):
    return jax.shard_map(
        shards,
        mesh=mesh,
        in_specs=(
            P(("scene", "view"), None),
            P(("scene", "view"), None),
            P(("scene", "view"), None),
            P(("scene", "view"), None),
            P(None, None, None, "view"),
            P(None, None, "view"),
            P(),
            P(),
        ),
        out_specs=P(("scene", "view"), None),
        check_vma=False,
    )
```

```python
import jax
import jax.numpy as jnp
from jax import lax
from jax.experimental import pallas as pl
from jax.experimental.pallas import tpu as pltpu
from jax.sharding import PartitionSpec as P

NS_STEPS = 5
GROUP = 16
PAIRS = GROUP // 2
DH = 64
HID = 1024
LANES = 128
COLS = 256

poly_one = 3.4445
poly_two = -4.775
poly_three = 2.0315

ROWS_BY_ROWS = (((1,), (1,)), ((), ()))
COLS_BY_COLS = (((0,), (0,)), ((), ()))


def plain_dot(left, right):
    return jnp.dot(left, right, preferred_element_type=jnp.float32)


def nt_dot(left, right):
    return lax.dot_general(left, right, ROWS_BY_ROWS, preferred_element_type=jnp.float32)


def side_by_side(left, right):
    return jnp.concatenate([left, right], axis=1)


def clear_grads(grad):
    grad[...] = jnp.zeros_like(grad)


def unpack_weights(pair, recv_w, weight):
    even, odd = recv_w[2 * pair], recv_w[2 * pair + 1]
    cols = pl.ds(pl.multiple_of(pair * LANES, LANES), LANES)
    weight[0, :, cols] = side_by_side(even[:DH, :DH], odd[:DH, :DH])
    weight[1, :, cols] = side_by_side(even[:DH, DH:], odd[:DH, DH:])
    weight[2, : DH // 2, cols] = side_by_side(even[DH:, :DH], odd[DH:, :DH])
    weight[2, DH // 2 :, cols] = side_by_side(even[DH:, DH:], odd[DH:, DH:])


def make_terms(slot, cols, keys, errors, weight, terms):
    gate = plain_dot(keys, weight[0, :, cols])
    up = plain_dot(keys, weight[1, :, cols])
    back = plain_dot(errors, weight[2, :, cols])
    sigma = 0.5 * jnp.tanh(0.5 * gate) + 0.5
    gated = gate * sigma
    terms[slot, 0, :, cols] = (back * up * (sigma + gated * (1.0 - sigma))).astype(jnp.bfloat16)
    terms[slot, 1, :, cols] = (back * gated).astype(jnp.bfloat16)
    terms[slot, 2, :, cols] = (gated * up).astype(jnp.bfloat16)


def add_grads(slot, cols, turned, terms, grad):
    grad[0, :, cols] += plain_dot(turned[slot, :DH, :], terms[slot, 0, :, cols])
    grad[1, :, cols] += plain_dot(turned[slot, :DH, :], terms[slot, 1, :, cols])
    grad[2, :, cols] += plain_dot(turned[slot, DH:, :], terms[slot, 2, :, cols])


def grad_chunk(pair, slot, recv_t, weight, turned, terms, grad, fill=True, drain=True):
    if fill:
        block = recv_t[pl.ds(2 * pair, 2)].reshape(2 * LANES, LANES)
        turned[slot] = block.T
        keys, errors = block[:, :DH], block[:, DH:]
    for at in range(HID // COLS):
        cols = slice(at * COLS, (at + 1) * COLS)
        if fill:
            make_terms(slot, cols, keys, errors, weight, terms)
        if drain:
            add_grads(1 - slot, cols, turned, terms, grad)


def split_three(value):
    high = value.astype(jnp.bfloat16)
    rest = value - high.astype(jnp.float32)
    middle = rest.astype(jnp.bfloat16)
    low = (rest - middle.astype(jnp.float32)).astype(jnp.bfloat16)
    return high, middle, low


def twin(value):
    return side_by_side(value, value)


def first_half(shape):
    return lax.broadcasted_iota(jnp.int32, shape, 1) < DH


def exact_twins(left, right):
    high, middle, low = left
    near = first_half(high.shape)
    wide = jnp.concatenate(
        [high, jnp.where(near, middle, high), jnp.where(near, middle, low)], axis=1
    )
    high, middle, low = right
    tall = jnp.concatenate([high, middle, high, low, middle, high], axis=0)
    return plain_dot(wide, tall)


def start_gram(part):
    high, middle, low = part
    stacked = jnp.concatenate([high, middle, low], axis=0)
    blocks = nt_dot(stacked, stacked)
    main = blocks[:DH, :LANES] + blocks[DH : 2 * DH, :LANES]
    side = blocks[2 * DH :, :DH] + blocks[:DH, 2 * DH :]
    return twin(main[:, :DH] + (main[:, DH:] + side))


def orthogonalizers(pieces):
    shape = (DH, 2 * DH)
    row = lax.broadcasted_iota(jnp.int32, shape, 0)
    eye = (row == lax.broadcasted_iota(jnp.int32, shape, 1) % DH).astype(jnp.float32)
    grams, totals = [], []
    for part in pieces:
        gram = start_gram(part)
        square_norm = 0.5 * jnp.sum(gram * eye, axis=(0, 1), keepdims=True)
        factor = 1.0 / (jnp.sqrt(square_norm) + 1e-07)
        grams.append(gram * (factor * factor))
        totals.append(factor)
    for step in range(NS_STEPS):
        cut = [split_three(gram) for gram in grams]
        squares = [exact_twins(one, one) for one in cut]
        blends = [
            poly_one * eye + poly_two * gram + poly_three * square
            for gram, square in zip(grams, squares)
        ]
        cut_blends = [split_three(blend) for blend in blends]
        if step < NS_STEPS - 1:
            cubes = [exact_twins(one, split_three(square)) for one, square in zip(cut, squares)]
            halves = [
                poly_one * gram + poly_two * square + poly_three * cube
                for gram, square, cube in zip(grams, squares, cubes)
            ]
            grams = [
                exact_twins(split_three(half), blend) for half, blend in zip(halves, cut_blends)
            ]
        totals = [
            blend * total if step == 0 else exact_twins(cut_blend, split_three(total))
            for blend, cut_blend, total in zip(blends, cut_blends, totals)
        ]
    return totals


def renew(grad, weight, fresh, turned_down, step_size):
    pieces = [split_three(grad[part]) for part in range(3)]
    totals = orthogonalizers(pieces)
    for part in range(3):
        high, middle, _ = split_three(totals[part])
        right = jnp.concatenate([pieces[part][0], pieces[part][1]] * 2, axis=0)
        start = weight[part].astype(jnp.float32)
        moved = start - step_size * plain_dot(side_by_side(high, middle), right)
        keep = jnp.sum(start * start, axis=0, keepdims=True)
        length = jnp.sum(moved * moved, axis=0, keepdims=True)
        moved = (moved * (jnp.sqrt(keep) / (jnp.sqrt(length) + 1e-06))).astype(jnp.bfloat16)
        if part < 2:
            fresh[part] = moved
        else:
            turned_down[...] = moved.T


SOURCES = 4


def apply_block(at, recv_q, fresh, turned_down, gain, send_o):
    take = pl.ds(at * SOURCES, SOURCES)
    count = SOURCES * DH // 2
    block = jnp.concatenate(
        [recv_q[take, :, :DH].reshape(count, DH), recv_q[take, :, DH:].reshape(count, DH)], axis=0
    )
    hidden = []
    for part in range(HID // COLS):
        cols = slice(part * COLS, (part + 1) * COLS)
        gate = plain_dot(block, fresh[0, :, cols])
        up = plain_dot(block, fresh[1, :, cols])
        sigma = 0.5 * jnp.tanh(0.5 * gate) + 0.5
        hidden.append((gate * sigma * up).astype(jnp.bfloat16))
    head_out = plain_dot(jnp.concatenate(hidden, axis=1), turned_down[...])
    mean_square = jnp.sum(head_out * head_out, axis=1, keepdims=True) * (1.0 / DH)
    done = head_out * lax.rsqrt(mean_square + 1e-06) * gain
    packed = side_by_side(done[:count], done[count:]).astype(jnp.bfloat16)
    send_o[take] = packed.reshape(SOURCES, DH // 2, LANES)


def pack_tokens(keys, values, rates, send_t):
    head_of = lax.broadcasted_iota(jnp.int32, (GROUP, LANES), 1) // DH
    row = lax.broadcasted_iota(jnp.int32, (GROUP, LANES), 0)
    for pair in range(PAIRS):
        cols = slice(pair * LANES, (pair + 1) * LANES)
        spread = (row == head_of + 2 * pair).astype(jnp.bfloat16)
        rate = lax.dot_general(
            rates[...], spread, COLS_BY_COLS, preferred_element_type=jnp.float32
        )
        error = (-(rate * values[:, cols].astype(jnp.float32))).astype(jnp.bfloat16)
        key = keys[:, cols]
        send_t[2 * pair] = side_by_side(key[:, :DH], error[:, :DH])
        send_t[2 * pair + 1] = side_by_side(key[:, DH:], error[:, DH:])


def pack_queries(queries, send_q):
    half = DH // 2
    for pair in range(PAIRS):
        cols = slice(pair * LANES, (pair + 1) * LANES)
        top, bottom = queries[:half, cols], queries[half:, cols]
        send_q[2 * pair] = side_by_side(top[:, :DH], bottom[:, :DH])
        send_q[2 * pair + 1] = side_by_side(top[:, DH:], bottom[:, DH:])


def pack_weights(gate_up, down_t, send_w):
    for head in range(GROUP):
        send_w[head, :DH, :] = side_by_side(gate_up[0, head], gate_up[1, head])
        down = down_t[head]
        send_w[head, DH:, :] = side_by_side(down[: DH // 2], down[DH // 2 :])


def whole_kernel(
    keys_hbm,
    values_hbm,
    rates_hbm,
    queries_hbm,
    gate_up_hbm,
    down_t_hbm,
    steps_hbm,
    gain_hbm,
    outputs,
    keys,
    values,
    rates,
    queries,
    gate_up,
    down_t,
    step_sizes,
    gain_rows,
    send_w,
    recv_w,
    send_t,
    recv_t,
    send_q,
    recv_q,
    send_o,
    recv_o,
    weight,
    turned,
    terms,
    grad,
    fresh,
    turned_down,
    out_sems,
    in_sems,
    here,
    loaded,
):
    me = lax.axis_index("view")
    my_pair, my_side = me // 2, me % 2
    my_row, my_depth = me // 4, my_pair % 2
    partner = 2 * my_pair + 1 - my_side

    def peer(step):
        return lax.rem(me + step, GROUP)

    def chip(rows, depth):
        return ((my_row + rows) % 4) * 2 + (my_depth + depth) % 2

    def loop(first, count, one):
        def loop_body(at, carry):
            one(at)
            return carry

        lax.fori_loop(first, count, loop_body, 0)

    loads = [
        pltpu.make_async_copy(far, near, loaded.at[at])
        for at, (far, near) in enumerate(
            (
                (gate_up_hbm, gate_up),
                (down_t_hbm, down_t),
                (keys_hbm, keys),
                (values_hbm, values),
                (rates_hbm, rates),
                (queries_hbm, queries),
                (steps_hbm, step_sizes),
                (gain_hbm, gain_rows),
            )
        )
    ]
    for load in loads:
        load.start()

    barrier = pltpu.get_barrier_semaphore()

    def greet(target):
        pl.semaphore_signal(
            barrier, inc=1, device_id={"view": target}, device_id_type=pl.DeviceIdType.MESH
        )

    for rows in (2, 1, 3, 0):
        for depth in (1, 0):
            if rows or depth:
                greet(2 * chip(rows, depth))
                greet(2 * chip(rows, depth) + 1)
    greet(partner)

    T_ORDER = [(3, 0), (1, 1), (3, 1), (1, 0), (2, 0), (0, 1), (2, 1)]
    W_ORDER = [(3, 0), (1, 1), (3, 1), (1, 0), (2, 0), (0, 1), (2, 1)]

    def to_all(build, order=W_ORDER):
        build(partner, me).start()
        for rows, depth in order:
            pair = chip(-rows % 4, depth)
            build(2 * pair, me).start()
            build(2 * pair + 1, me).start()

    def copy(kind, source, target_buffer):
        def build(target, origin):
            return pltpu.make_async_remote_copy(
                src_ref=source.at[target],
                dst_ref=target_buffer.at[origin],
                send_sem=out_sems.at[kind, target],
                recv_sem=in_sems.at[kind, origin],
                device_id={"view": target},
                device_id_type=pl.DeviceIdType.MESH,
            )

        return build

    w_copy = copy(0, send_w, recv_w)
    t_copy = copy(1, send_t, recv_t)
    q_copy = copy(2, send_q, recv_q)
    o_copy = copy(3, send_o, recv_o)

    for load in loads[:2]:
        load.wait()
    pack_weights(gate_up, down_t, send_w)
    for load in loads[2:5]:
        load.wait()
    pack_tokens(keys, values, rates, send_t)
    for load in loads[5:]:
        load.wait()
    pack_queries(queries, send_q)
    pl.semaphore_wait(barrier, GROUP - 1)
    to_all(w_copy)
    to_all(t_copy, T_ORDER)

    own = [
        pltpu.make_async_copy(source.at[me], target.at[me], here.at[at])
        for at, (source, target) in enumerate(
            ((send_w, recv_w), (send_t, recv_t), (send_q, recv_q))
        )
    ]
    for copied in own:
        copied.start()
    clear_grads(grad)
    for copied in own:
        copied.wait()

    loop(1, GROUP, lambda step: w_copy(peer(step), peer(step)).wait_recv())
    for pair in range(PAIRS):
        unpack_weights(pair, recv_w, weight)

    def take_tokens(step):
        pair = chip(*T_ORDER[step])
        t_copy(2 * pair, 2 * pair).wait_recv()
        t_copy(2 * pair + 1, 2 * pair + 1).wait_recv()
        return pair

    t_copy(partner, partner).wait_recv()
    grad_chunk(my_pair, 0, recv_t, weight, turned, terms, grad, drain=False)
    for step in range(7):
        grad_chunk(take_tokens(step), 1 - step % 2, recv_t, weight, turned, terms, grad)
        if step == 1:
            to_all(q_copy)
    grad_chunk(0, 0, recv_t, weight, turned, terms, grad, fill=False)

    renew(grad, weight, fresh, turned_down, step_sizes[me])
    gain = gain_rows[pl.ds(my_pair, 1), :]
    gain = jnp.where(my_side == 0, gain[:, :DH], gain[:, DH:])

    loop(1, GROUP, lambda step: q_copy(peer(step), peer(step)).wait_recv())
    for rows in (2, 1, 3, 0):
        block = (my_row + rows) % 4
        apply_block(block, recv_q, fresh, turned_down, gain, send_o)
        for depth in (1, 0):
            pair = chip(rows, depth)
            if rows or depth:
                o_copy(2 * pair, me).start()
                o_copy(2 * pair + 1, me).start()
    o_copy(partner, me).start()
    own_o = pltpu.make_async_copy(send_o.at[me], recv_o.at[me], here.at[3])
    own_o.start()

    def finish_sends(step):
        for build in (w_copy, t_copy, q_copy, o_copy):
            build(peer(step), me).wait_send()

    loop(1, GROUP, finish_sends)
    own_o.wait()
    half = DH // 2
    for rows in (2, 3, 1, 0):
        for depth in range(2):
            pair = chip(rows, depth)
            for side in range(2):
                if rows or depth:
                    o_copy(2 * pair + side, 2 * pair + side).wait_recv()
                elif side:
                    o_copy(partner, partner).wait_recv()
            even, odd = recv_o[2 * pair], recv_o[2 * pair + 1]
            cols = pl.ds(pl.multiple_of(pair * LANES, LANES), LANES)
            outputs[:half, cols] = side_by_side(even[:, :DH], odd[:, :DH])
            outputs[half:, cols] = side_by_side(even[:, DH:], odd[:, DH:])


def shards(keys, values, rates, queries, gate_up, down_t, step_sizes, gain):
    bf16, f32 = jnp.bfloat16, jnp.float32

    def boxes(rows):
        return [pltpu.VMEM((GROUP, rows, LANES), bf16)] * 2

    return pl.pallas_call(
        whole_kernel,
        out_shape=pltpu.VMEM(queries.shape, bf16),
        in_specs=[pl.BlockSpec(memory_space=pltpu.HBM)] * 8,
        out_specs=pl.BlockSpec(memory_space=pltpu.VMEM),
        scratch_shapes=[
            pltpu.VMEM(keys.shape, bf16),
            pltpu.VMEM(values.shape, bf16),
            pltpu.VMEM(rates.shape[::-1], bf16),
            pltpu.VMEM(queries.shape, bf16),
            pltpu.VMEM(gate_up.shape, bf16),
            pltpu.VMEM(down_t.shape, bf16),
            pltpu.SMEM(step_sizes.shape, f32),
            pltpu.VMEM((PAIRS, LANES), f32),
        ]
        + boxes(DH + DH // 2)
        + boxes(LANES)
        + boxes(DH // 2)
        + boxes(DH // 2)
        + [
            pltpu.VMEM((3, DH, HID), bf16),
            pltpu.VMEM((2, 2 * DH, 2 * LANES), bf16),
            pltpu.VMEM((2, 3, 2 * LANES, HID), bf16),
            pltpu.VMEM((3, DH, HID), f32),
            pltpu.VMEM((2, DH, HID), bf16),
            pltpu.VMEM((HID, DH), bf16),
            pltpu.SemaphoreType.DMA((4, GROUP)),
            pltpu.SemaphoreType.DMA((4, GROUP)),
            pltpu.SemaphoreType.DMA((4,)),
            pltpu.SemaphoreType.DMA((8,)),
        ],
        compiler_params=pltpu.CompilerParams(
            collective_id=0, has_side_effects=True, vmem_limit_bytes=60 << 20
        ),
    )(
        keys,
        values,
        rates.T,
        queries,
        gate_up,
        down_t,
        step_sizes,
        gain.reshape(PAIRS, LANES),
    )


def solution(mesh):
    return jax.shard_map(
        shards,
        mesh=mesh,
        in_specs=(
            P(("scene", "view"), None),
            P(("scene", "view"), None),
            P(("scene", "view"), None),
            P(("scene", "view"), None),
            P(None, None, None, "view"),
            P(None, None, "view"),
            P(),
            P(),
        ),
        out_specs=P(("scene", "view"), None),
        check_vma=False,
    )
```

```python
import jax
import jax.numpy as jnp
from jax import lax
from jax.experimental import pallas as pl
from jax.experimental.pallas import tpu as pltpu
from jax.sharding import PartitionSpec as P

NS_STEPS = 5
GROUP = 16
PAIRS = GROUP // 2
DH = 64
HID = 1024
LANES = 128
COLS = 256

poly_one = 3.4445
poly_two = -4.775
poly_three = 2.0315

ROWS_BY_ROWS = (((1,), (1,)), ((), ()))
COLS_BY_COLS = (((0,), (0,)), ((), ()))


def plain_dot(left, right):
    return jnp.dot(left, right, preferred_element_type=jnp.float32)


def nt_dot(left, right):
    return lax.dot_general(left, right, ROWS_BY_ROWS, preferred_element_type=jnp.float32)


def side_by_side(left, right):
    return jnp.concatenate([left, right], axis=1)


def clear_grads(grad):
    grad[...] = jnp.zeros_like(grad)


def unpack_weights(pair, recv_w, weight):
    even, odd = recv_w[2 * pair], recv_w[2 * pair + 1]
    cols = pl.ds(pl.multiple_of(pair * LANES, LANES), LANES)
    weight[0, :, cols] = side_by_side(even[:DH, :DH], odd[:DH, :DH])
    weight[1, :, cols] = side_by_side(even[:DH, DH:], odd[:DH, DH:])
    weight[2, : DH // 2, cols] = side_by_side(even[DH:, :DH], odd[DH:, :DH])
    weight[2, DH // 2 :, cols] = side_by_side(even[DH:, DH:], odd[DH:, DH:])


def make_terms(slot, cols, keys, errors, weight, terms):
    gate = plain_dot(keys, weight[0, :, cols])
    up = plain_dot(keys, weight[1, :, cols])
    back = plain_dot(errors, weight[2, :, cols])
    sigma = 0.5 * jnp.tanh(0.5 * gate) + 0.5
    gated = gate * sigma
    terms[slot, 0, :, cols] = (back * up * (sigma + gated * (1.0 - sigma))).astype(jnp.bfloat16)
    terms[slot, 1, :, cols] = (back * gated).astype(jnp.bfloat16)
    terms[slot, 2, :, cols] = (gated * up).astype(jnp.bfloat16)


def add_grads(slot, cols, turned, terms, grad):
    grad[0, :, cols] += plain_dot(turned[slot, :DH, :], terms[slot, 0, :, cols])
    grad[1, :, cols] += plain_dot(turned[slot, :DH, :], terms[slot, 1, :, cols])
    grad[2, :, cols] += plain_dot(turned[slot, DH:, :], terms[slot, 2, :, cols])


def grad_chunk(pair, slot, recv_t, weight, turned, terms, grad, fill=True, drain=True):
    if fill:
        block = recv_t[pl.ds(2 * pair, 2)].reshape(2 * LANES, LANES)
        turned[slot] = block.T
        keys, errors = block[:, :DH], block[:, DH:]
    for at in range(HID // COLS):
        cols = slice(at * COLS, (at + 1) * COLS)
        if fill:
            make_terms(slot, cols, keys, errors, weight, terms)
        if drain:
            add_grads(1 - slot, cols, turned, terms, grad)


def split_three(value):
    high = value.astype(jnp.bfloat16)
    rest = value - high.astype(jnp.float32)
    middle = rest.astype(jnp.bfloat16)
    low = (rest - middle.astype(jnp.float32)).astype(jnp.bfloat16)
    return high, middle, low


def twin(value):
    return side_by_side(value, value)


def first_half(shape):
    return lax.broadcasted_iota(jnp.int32, shape, 1) < DH


def exact_twins(left, right):
    high, middle, low = left
    near = first_half(high.shape)
    wide = jnp.concatenate(
        [high, jnp.where(near, middle, high), jnp.where(near, middle, low)], axis=1
    )
    high, middle, low = right
    tall = jnp.concatenate([high, middle, high, low, middle, high], axis=0)
    return plain_dot(wide, tall)


def start_gram(part):
    high, middle, low = part
    stacked = jnp.concatenate([high, middle, low], axis=0)
    blocks = nt_dot(stacked, stacked)
    main = blocks[:DH, :LANES] + blocks[DH : 2 * DH, :LANES]
    side = blocks[2 * DH :, :DH] + blocks[:DH, 2 * DH :]
    return twin(main[:, :DH] + (main[:, DH:] + side))


def orthogonalizers(pieces):
    shape = (DH, 2 * DH)
    row = lax.broadcasted_iota(jnp.int32, shape, 0)
    eye = (row == lax.broadcasted_iota(jnp.int32, shape, 1) % DH).astype(jnp.float32)
    grams, totals = [], []
    for part in pieces:
        gram = start_gram(part)
        square_norm = 0.5 * jnp.sum(gram * eye, axis=(0, 1), keepdims=True)
        factor = 1.0 / (jnp.sqrt(square_norm) + 1e-07)
        grams.append(gram * (factor * factor))
        totals.append(factor)
    for step in range(NS_STEPS):
        cut = [split_three(gram) for gram in grams]
        squares = [exact_twins(one, one) for one in cut]
        blends = [
            poly_one * eye + poly_two * gram + poly_three * square
            for gram, square in zip(grams, squares)
        ]
        cut_blends = [split_three(blend) for blend in blends]
        if step < NS_STEPS - 1:
            cubes = [exact_twins(one, split_three(square)) for one, square in zip(cut, squares)]
            halves = [
                poly_one * gram + poly_two * square + poly_three * cube
                for gram, square, cube in zip(grams, squares, cubes)
            ]
            grams = [
                exact_twins(split_three(half), blend) for half, blend in zip(halves, cut_blends)
            ]
        totals = [
            blend * total if step == 0 else exact_twins(cut_blend, split_three(total))
            for blend, cut_blend, total in zip(blends, cut_blends, totals)
        ]
    return totals


def renew(grad, weight, fresh, turned_down, step_size):
    pieces = [split_three(grad[part]) for part in range(3)]
    totals = orthogonalizers(pieces)
    for part in range(3):
        high, middle, _ = split_three(totals[part])
        right = jnp.concatenate([pieces[part][0], pieces[part][1]] * 2, axis=0)
        start = weight[part].astype(jnp.float32)
        moved = start - step_size * plain_dot(side_by_side(high, middle), right)
        keep = jnp.sum(start * start, axis=0, keepdims=True)
        length = jnp.sum(moved * moved, axis=0, keepdims=True)
        moved = (moved * (jnp.sqrt(keep) / (jnp.sqrt(length) + 1e-06))).astype(jnp.bfloat16)
        if part < 2:
            fresh[part] = moved
        else:
            turned_down[...] = moved.T


SOURCES = 4


def apply_block(at, recv_q, fresh, turned_down, gain, send_o):
    take = pl.ds(at * SOURCES, SOURCES)
    count = SOURCES * DH // 2
    block = jnp.concatenate(
        [recv_q[take, :, :DH].reshape(count, DH), recv_q[take, :, DH:].reshape(count, DH)], axis=0
    )
    hidden = []
    for part in range(HID // COLS):
        cols = slice(part * COLS, (part + 1) * COLS)
        gate = plain_dot(block, fresh[0, :, cols])
        up = plain_dot(block, fresh[1, :, cols])
        sigma = 0.5 * jnp.tanh(0.5 * gate) + 0.5
        hidden.append((gate * sigma * up).astype(jnp.bfloat16))
    head_out = plain_dot(jnp.concatenate(hidden, axis=1), turned_down[...])
    mean_square = jnp.sum(head_out * head_out, axis=1, keepdims=True) * (1.0 / DH)
    done = head_out * lax.rsqrt(mean_square + 1e-06) * gain
    packed = side_by_side(done[:count], done[count:]).astype(jnp.bfloat16)
    send_o[take] = packed.reshape(SOURCES, DH // 2, LANES)


def pack_tokens(keys, values, rates, send_t):
    head_of = lax.broadcasted_iota(jnp.int32, (GROUP, LANES), 1) // DH
    row = lax.broadcasted_iota(jnp.int32, (GROUP, LANES), 0)
    for pair in range(PAIRS):
        cols = slice(pair * LANES, (pair + 1) * LANES)
        spread = (row == head_of + 2 * pair).astype(jnp.bfloat16)
        rate = lax.dot_general(
            rates[...], spread, COLS_BY_COLS, preferred_element_type=jnp.float32
        )
        error = (-(rate * values[:, cols].astype(jnp.float32))).astype(jnp.bfloat16)
        key = keys[:, cols]
        send_t[2 * pair] = side_by_side(key[:, :DH], error[:, :DH])
        send_t[2 * pair + 1] = side_by_side(key[:, DH:], error[:, DH:])


def pack_queries(queries, send_q):
    half = DH // 2
    for pair in range(PAIRS):
        cols = slice(pair * LANES, (pair + 1) * LANES)
        top, bottom = queries[:half, cols], queries[half:, cols]
        send_q[2 * pair] = side_by_side(top[:, :DH], bottom[:, :DH])
        send_q[2 * pair + 1] = side_by_side(top[:, DH:], bottom[:, DH:])


def pack_weights(gate_up, down_t, send_w):
    for head in range(GROUP):
        send_w[head, :DH, :] = side_by_side(gate_up[0, head], gate_up[1, head])
        down = down_t[head]
        send_w[head, DH:, :] = side_by_side(down[: DH // 2], down[DH // 2 :])


def whole_kernel(
    keys_hbm,
    values_hbm,
    rates_hbm,
    queries_hbm,
    gate_up_hbm,
    down_t_hbm,
    steps_hbm,
    gain_hbm,
    outputs,
    keys,
    values,
    rates,
    queries,
    gate_up,
    down_t,
    step_sizes,
    gain_rows,
    send_w,
    recv_w,
    send_t,
    recv_t,
    send_q,
    recv_q,
    send_o,
    recv_o,
    weight,
    turned,
    terms,
    grad,
    fresh,
    turned_down,
    out_sems,
    in_sems,
    here,
    loaded,
):
    me = lax.axis_index("view")
    my_pair, my_side = me // 2, me % 2
    my_row, my_depth = me // 4, my_pair % 2
    partner = 2 * my_pair + 1 - my_side

    def peer(step):
        return lax.rem(me + step, GROUP)

    def chip(rows, depth):
        return ((my_row + rows) % 4) * 2 + (my_depth + depth) % 2

    def loop(first, count, one):
        def loop_body(at, carry):
            one(at)
            return carry

        lax.fori_loop(first, count, loop_body, 0)

    loads = [
        pltpu.make_async_copy(far, near, loaded.at[at])
        for at, (far, near) in enumerate(
            (
                (gate_up_hbm, gate_up),
                (down_t_hbm, down_t),
                (keys_hbm, keys),
                (values_hbm, values),
                (rates_hbm, rates),
                (queries_hbm, queries),
                (steps_hbm, step_sizes),
                (gain_hbm, gain_rows),
            )
        )
    ]
    for load in loads:
        load.start()

    barrier = pltpu.get_barrier_semaphore()

    def greet(target):
        pl.semaphore_signal(
            barrier, inc=1, device_id={"view": target}, device_id_type=pl.DeviceIdType.MESH
        )

    for rows in (2, 1, 3, 0):
        for depth in (1, 0):
            if rows or depth:
                greet(2 * chip(rows, depth))
                greet(2 * chip(rows, depth) + 1)
    greet(partner)

    T_ORDER = [(3, 0), (1, 0), (0, 1), (3, 1), (1, 1), (2, 0), (2, 1)]
    W_SENT = [(3, 0, 0), (1, 1, 0), (3, 0, 1), (1, 1, 1), (3, 1, 0), (1, 0, 0), (3, 1, 1), (1, 0, 1), (2, 0, 0), (0, 1, 0), (2, 0, 1), (0, 1, 1), (2, 1, 0), (2, 1, 1)]
    T_SENT = [(3, 0, 0), (1, 0, 0), (0, 1, 0), (3, 0, 1), (1, 0, 1), (0, 1, 1), (3, 1, 0), (1, 1, 0), (3, 1, 1), (1, 1, 1), (2, 0, 0), (2, 1, 0), (2, 0, 1), (2, 1, 1)]
    W_ORDER = [(3, 0), (1, 1), (3, 1), (1, 0), (2, 0), (0, 1), (2, 1)]

    def send_to(build, places):
        for rows, depth, side in places:
            build(2 * chip(-rows % 4, depth) + side, me).start()

    def to_all(build, order=None):
        build(partner, me).start()
        send_to(build, W_SENT if order is None else T_SENT)

    def copy(kind, source, target_buffer):
        def build(target, origin):
            return pltpu.make_async_remote_copy(
                src_ref=source.at[target],
                dst_ref=target_buffer.at[origin],
                send_sem=out_sems.at[kind, target],
                recv_sem=in_sems.at[kind, origin],
                device_id={"view": target},
                device_id_type=pl.DeviceIdType.MESH,
            )

        return build

    w_copy = copy(0, send_w, recv_w)
    t_copy = copy(1, send_t, recv_t)
    q_copy = copy(2, send_q, recv_q)
    o_copy = copy(3, send_o, recv_o)

    for load in loads[:2]:
        load.wait()
    pack_weights(gate_up, down_t, send_w)
    for load in loads[2:5]:
        load.wait()
    pack_tokens(keys, values, rates, send_t)
    for load in loads[5:]:
        load.wait()
    pack_queries(queries, send_q)
    pl.semaphore_wait(barrier, GROUP - 1)
    to_all(w_copy)
    to_all(t_copy, T_ORDER)

    own = [
        pltpu.make_async_copy(source.at[me], target.at[me], here.at[at])
        for at, (source, target) in enumerate(
            ((send_w, recv_w), (send_t, recv_t), (send_q, recv_q))
        )
    ]
    for copied in own:
        copied.start()
    clear_grads(grad)
    for copied in own:
        copied.wait()

    loop(1, GROUP, lambda step: w_copy(peer(step), peer(step)).wait_recv())
    for pair in range(PAIRS):
        unpack_weights(pair, recv_w, weight)

    def take_tokens(step):
        pair = chip(*T_ORDER[step])
        t_copy(2 * pair, 2 * pair).wait_recv()
        t_copy(2 * pair + 1, 2 * pair + 1).wait_recv()
        return pair

    t_copy(partner, partner).wait_recv()
    grad_chunk(my_pair, 0, recv_t, weight, turned, terms, grad, drain=False)
    for step in range(7):
        grad_chunk(take_tokens(step), 1 - step % 2, recv_t, weight, turned, terms, grad)
        if step == 1:
            to_all(q_copy)
    grad_chunk(0, 0, recv_t, weight, turned, terms, grad, fill=False)

    renew(grad, weight, fresh, turned_down, step_sizes[me])
    gain = gain_rows[pl.ds(my_pair, 1), :]
    gain = jnp.where(my_side == 0, gain[:, :DH], gain[:, DH:])

    loop(1, GROUP, lambda step: q_copy(peer(step), peer(step)).wait_recv())
    for rows in (2, 1, 3, 0):
        block = (my_row + rows) % 4
        apply_block(block, recv_q, fresh, turned_down, gain, send_o)
        for depth in (1, 0):
            pair = chip(rows, depth)
            if rows or depth:
                o_copy(2 * pair, me).start()
                o_copy(2 * pair + 1, me).start()
    o_copy(partner, me).start()
    own_o = pltpu.make_async_copy(send_o.at[me], recv_o.at[me], here.at[3])
    own_o.start()

    def finish_sends(step):
        for build in (w_copy, t_copy, q_copy, o_copy):
            build(peer(step), me).wait_send()

    loop(1, GROUP, finish_sends)
    own_o.wait()
    half = DH // 2
    for rows in (2, 3, 1, 0):
        for depth in range(2):
            pair = chip(rows, depth)
            for side in range(2):
                if rows or depth:
                    o_copy(2 * pair + side, 2 * pair + side).wait_recv()
                elif side:
                    o_copy(partner, partner).wait_recv()
            even, odd = recv_o[2 * pair], recv_o[2 * pair + 1]
            cols = pl.ds(pl.multiple_of(pair * LANES, LANES), LANES)
            outputs[:half, cols] = side_by_side(even[:, :DH], odd[:, :DH])
            outputs[half:, cols] = side_by_side(even[:, DH:], odd[:, DH:])


def shards(keys, values, rates, queries, gate_up, down_t, step_sizes, gain):
    bf16, f32 = jnp.bfloat16, jnp.float32

    def boxes(rows):
        return [pltpu.VMEM((GROUP, rows, LANES), bf16)] * 2

    return pl.pallas_call(
        whole_kernel,
        out_shape=pltpu.VMEM(queries.shape, bf16),
        in_specs=[pl.BlockSpec(memory_space=pltpu.HBM)] * 8,
        out_specs=pl.BlockSpec(memory_space=pltpu.VMEM),
        scratch_shapes=[
            pltpu.VMEM(keys.shape, bf16),
            pltpu.VMEM(values.shape, bf16),
            pltpu.VMEM(rates.shape[::-1], bf16),
            pltpu.VMEM(queries.shape, bf16),
            pltpu.VMEM(gate_up.shape, bf16),
            pltpu.VMEM(down_t.shape, bf16),
            pltpu.SMEM(step_sizes.shape, f32),
            pltpu.VMEM((PAIRS, LANES), f32),
        ]
        + boxes(DH + DH // 2)
        + boxes(LANES)
        + boxes(DH // 2)
        + boxes(DH // 2)
        + [
            pltpu.VMEM((3, DH, HID), bf16),
            pltpu.VMEM((2, 2 * DH, 2 * LANES), bf16),
            pltpu.VMEM((2, 3, 2 * LANES, HID), bf16),
            pltpu.VMEM((3, DH, HID), f32),
            pltpu.VMEM((2, DH, HID), bf16),
            pltpu.VMEM((HID, DH), bf16),
            pltpu.SemaphoreType.DMA((4, GROUP)),
            pltpu.SemaphoreType.DMA((4, GROUP)),
            pltpu.SemaphoreType.DMA((4,)),
            pltpu.SemaphoreType.DMA((8,)),
        ],
        compiler_params=pltpu.CompilerParams(
            collective_id=0, has_side_effects=True, vmem_limit_bytes=60 << 20
        ),
    )(
        keys,
        values,
        rates.T,
        queries,
        gate_up,
        down_t,
        step_sizes,
        gain.reshape(PAIRS, LANES),
    )


def solution(mesh):
    return jax.shard_map(
        shards,
        mesh=mesh,
        in_specs=(
            P(("scene", "view"), None),
            P(("scene", "view"), None),
            P(("scene", "view"), None),
            P(("scene", "view"), None),
            P(None, None, None, "view"),
            P(None, None, "view"),
            P(),
            P(),
        ),
        out_specs=P(("scene", "view"), None),
        check_vma=False,
    )
```

```python
import jax
import jax.numpy as jnp
from jax import lax
from jax.experimental import pallas as pl
from jax.experimental.pallas import tpu as pltpu
from jax.sharding import PartitionSpec as P

NS_STEPS = 5
GROUP = 16
PAIRS = GROUP // 2
DH = 64
HID = 1024
LANES = 128
COLS = 256

poly_one = 3.4445
poly_two = -4.775
poly_three = 2.0315

ROWS_BY_ROWS = (((1,), (1,)), ((), ()))
COLS_BY_COLS = (((0,), (0,)), ((), ()))


def plain_dot(left, right):
    return jnp.dot(left, right, preferred_element_type=jnp.float32)


def nt_dot(left, right):
    return lax.dot_general(left, right, ROWS_BY_ROWS, preferred_element_type=jnp.float32)


def side_by_side(left, right):
    return jnp.concatenate([left, right], axis=1)


def clear_grads(grad):
    grad[...] = jnp.zeros_like(grad)


def unpack_weights(pair, recv_w, weight):
    even, odd = recv_w[2 * pair], recv_w[2 * pair + 1]
    cols = pl.ds(pl.multiple_of(pair * LANES, LANES), LANES)
    weight[0, :, cols] = side_by_side(even[:DH, :DH], odd[:DH, :DH])
    weight[1, :, cols] = side_by_side(even[:DH, DH:], odd[:DH, DH:])
    weight[2, : DH // 2, cols] = side_by_side(even[DH:, :DH], odd[DH:, :DH])
    weight[2, DH // 2 :, cols] = side_by_side(even[DH:, DH:], odd[DH:, DH:])


def make_terms(slot, cols, keys, errors, weight, terms):
    gate = plain_dot(keys, weight[0, :, cols])
    up = plain_dot(keys, weight[1, :, cols])
    back = plain_dot(errors, weight[2, :, cols])
    sigma = 0.5 * jnp.tanh(0.5 * gate) + 0.5
    gated = gate * sigma
    terms[slot, 0, :, cols] = (back * up * (sigma + gated * (1.0 - sigma))).astype(jnp.bfloat16)
    terms[slot, 1, :, cols] = (back * gated).astype(jnp.bfloat16)
    terms[slot, 2, :, cols] = (gated * up).astype(jnp.bfloat16)


def add_grads(slot, cols, turned, terms, grad):
    grad[0, :, cols] += plain_dot(turned[slot, :DH, :], terms[slot, 0, :, cols])
    grad[1, :, cols] += plain_dot(turned[slot, :DH, :], terms[slot, 1, :, cols])
    grad[2, :, cols] += plain_dot(turned[slot, DH:, :], terms[slot, 2, :, cols])


def grad_chunk(pair, slot, recv_t, weight, turned, terms, grad, fill=True, drain=True, last=False):
    if fill:
        block = recv_t[pl.ds(2 * pair, 2)].reshape(2 * LANES, LANES)
        turned[slot] = block.T
        keys, errors = block[:, :DH], block[:, DH:]
    for at in range(HID // COLS):
        cols = slice(at * COLS, (at + 1) * COLS)
        if fill:
            make_terms(slot, cols, keys, errors, weight, terms)
        if drain:
            add_grads(1 - slot, cols, turned, terms, grad)
        if last and at:
            add_grads(slot, slice((at - 1) * COLS, at * COLS), turned, terms, grad)
    if last:
        add_grads(slot, slice(HID - COLS, HID), turned, terms, grad)


def split_three(value):
    high = value.astype(jnp.bfloat16)
    rest = value - high.astype(jnp.float32)
    middle = rest.astype(jnp.bfloat16)
    low = (rest - middle.astype(jnp.float32)).astype(jnp.bfloat16)
    return high, middle, low


def twin(value):
    return side_by_side(value, value)


def first_half(shape):
    return lax.broadcasted_iota(jnp.int32, shape, 1) < DH


def exact_twins(left, right):
    high, middle, low = left
    near = first_half(high.shape)
    wide = jnp.concatenate(
        [high, jnp.where(near, middle, high), jnp.where(near, middle, low)], axis=1
    )
    high, middle, low = right
    tall = jnp.concatenate([high, middle, high, low, middle, high], axis=0)
    return plain_dot(wide, tall)


def start_gram(part):
    high, middle, low = part
    stacked = jnp.concatenate([high, middle, low], axis=0)
    blocks = nt_dot(stacked, stacked)
    main = blocks[:DH, :LANES] + blocks[DH : 2 * DH, :LANES]
    side = blocks[2 * DH :, :DH] + blocks[:DH, 2 * DH :]
    return twin(main[:, :DH] + (main[:, DH:] + side))


def orthogonalizers(pieces):
    shape = (DH, 2 * DH)
    row = lax.broadcasted_iota(jnp.int32, shape, 0)
    eye = (row == lax.broadcasted_iota(jnp.int32, shape, 1) % DH).astype(jnp.float32)
    grams, totals = [], []
    for part in pieces:
        gram = start_gram(part)
        square_norm = 0.5 * jnp.sum(gram * eye, axis=(0, 1), keepdims=True)
        factor = 1.0 / (jnp.sqrt(square_norm) + 1e-07)
        grams.append(gram * (factor * factor))
        totals.append(factor)
    for step in range(NS_STEPS):
        cut = [split_three(gram) for gram in grams]
        squares = [exact_twins(one, one) for one in cut]
        blends = [
            poly_one * eye + poly_two * gram + poly_three * square
            for gram, square in zip(grams, squares)
        ]
        cut_blends = [split_three(blend) for blend in blends]
        if step < NS_STEPS - 1:
            cubes = [exact_twins(one, split_three(square)) for one, square in zip(cut, squares)]
            halves = [
                poly_one * gram + poly_two * square + poly_three * cube
                for gram, square, cube in zip(grams, squares, cubes)
            ]
            grams = [
                exact_twins(split_three(half), blend) for half, blend in zip(halves, cut_blends)
            ]
        totals = [
            blend * total if step == 0 else exact_twins(cut_blend, split_three(total))
            for blend, cut_blend, total in zip(blends, cut_blends, totals)
        ]
    return totals


def renew(grad, weight, fresh, turned_down, step_size):
    pieces = [split_three(grad[part]) for part in range(3)]
    totals = orthogonalizers(pieces)
    for part in range(3):
        high, middle, _ = split_three(totals[part])
        right = jnp.concatenate([pieces[part][0], pieces[part][1]] * 2, axis=0)
        start = weight[part].astype(jnp.float32)
        moved = start - step_size * plain_dot(side_by_side(high, middle), right)
        keep = jnp.sum(start * start, axis=0, keepdims=True)
        length = jnp.sum(moved * moved, axis=0, keepdims=True)
        moved = (moved * (jnp.sqrt(keep) / (jnp.sqrt(length) + 1e-06))).astype(jnp.bfloat16)
        if part < 2:
            fresh[part] = moved
        else:
            turned_down[...] = moved.T


SOURCES = 4


def apply_block(at, recv_q, fresh, turned_down, gain, send_o):
    take = pl.ds(at * SOURCES, SOURCES)
    count = SOURCES * DH // 2
    block = jnp.concatenate(
        [recv_q[take, :, :DH].reshape(count, DH), recv_q[take, :, DH:].reshape(count, DH)], axis=0
    )
    hidden = []
    for part in range(HID // COLS):
        cols = slice(part * COLS, (part + 1) * COLS)
        gate = plain_dot(block, fresh[0, :, cols])
        up = plain_dot(block, fresh[1, :, cols])
        sigma = 0.5 * jnp.tanh(0.5 * gate) + 0.5
        hidden.append((gate * sigma * up).astype(jnp.bfloat16))
    head_out = plain_dot(jnp.concatenate(hidden, axis=1), turned_down[...])
    mean_square = jnp.sum(head_out * head_out, axis=1, keepdims=True) * (1.0 / DH)
    done = head_out * lax.rsqrt(mean_square + 1e-06) * gain
    packed = side_by_side(done[:count], done[count:]).astype(jnp.bfloat16)
    send_o[take] = packed.reshape(SOURCES, DH // 2, LANES)


def pack_tokens(keys, values, rates, send_t):
    head_of = lax.broadcasted_iota(jnp.int32, (GROUP, LANES), 1) // DH
    row = lax.broadcasted_iota(jnp.int32, (GROUP, LANES), 0)
    for pair in range(PAIRS):
        cols = slice(pair * LANES, (pair + 1) * LANES)
        spread = (row == head_of + 2 * pair).astype(jnp.bfloat16)
        rate = lax.dot_general(
            rates[...], spread, COLS_BY_COLS, preferred_element_type=jnp.float32
        )
        error = (-(rate * values[:, cols].astype(jnp.float32))).astype(jnp.bfloat16)
        key = keys[:, cols]
        send_t[2 * pair] = side_by_side(key[:, :DH], error[:, :DH])
        send_t[2 * pair + 1] = side_by_side(key[:, DH:], error[:, DH:])


def pack_queries(queries, send_q):
    half = DH // 2
    for pair in range(PAIRS):
        cols = slice(pair * LANES, (pair + 1) * LANES)
        top, bottom = queries[:half, cols], queries[half:, cols]
        send_q[2 * pair] = side_by_side(top[:, :DH], bottom[:, :DH])
        send_q[2 * pair + 1] = side_by_side(top[:, DH:], bottom[:, DH:])


def pack_weights(gate_up, down_t, send_w):
    for head in range(GROUP):
        send_w[head, :DH, :] = side_by_side(gate_up[0, head], gate_up[1, head])
        down = down_t[head]
        send_w[head, DH:, :] = side_by_side(down[: DH // 2], down[DH // 2 :])


def whole_kernel(
    keys_hbm,
    values_hbm,
    rates_hbm,
    queries_hbm,
    gate_up_hbm,
    down_t_hbm,
    steps_hbm,
    gain_hbm,
    outputs,
    keys,
    values,
    rates,
    queries,
    gate_up,
    down_t,
    step_sizes,
    gain_rows,
    send_w,
    recv_w,
    send_t,
    recv_t,
    send_q,
    recv_q,
    send_o,
    recv_o,
    weight,
    turned,
    terms,
    grad,
    fresh,
    turned_down,
    out_sems,
    in_sems,
    here,
    loaded,
):
    me = lax.axis_index("view")
    my_pair, my_side = me // 2, me % 2
    my_row, my_depth = me // 4, my_pair % 2
    partner = 2 * my_pair + 1 - my_side

    def peer(step):
        return lax.rem(me + step, GROUP)

    def chip(rows, depth):
        return ((my_row + rows) % 4) * 2 + (my_depth + depth) % 2

    def loop(first, count, one):
        def loop_body(at, carry):
            one(at)
            return carry

        lax.fori_loop(first, count, loop_body, 0)

    loads = [
        pltpu.make_async_copy(far, near, loaded.at[at])
        for at, (far, near) in enumerate(
            (
                (gate_up_hbm, gate_up),
                (down_t_hbm, down_t),
                (keys_hbm, keys),
                (values_hbm, values),
                (rates_hbm, rates),
                (queries_hbm, queries),
                (steps_hbm, step_sizes),
                (gain_hbm, gain_rows),
            )
        )
    ]
    for load in loads:
        load.start()

    barrier = pltpu.get_barrier_semaphore()

    def greet(target):
        pl.semaphore_signal(
            barrier, inc=1, device_id={"view": target}, device_id_type=pl.DeviceIdType.MESH
        )

    for rows in (2, 1, 3, 0):
        for depth in (1, 0):
            if rows or depth:
                greet(2 * chip(rows, depth))
                greet(2 * chip(rows, depth) + 1)
    greet(partner)

    T_ORDER = [(3, 0), (1, 0), (0, 1), (3, 1), (1, 1), (2, 0), (2, 1)]
    W_SENT = [(3, 0, 0), (1, 1, 0), (3, 0, 1), (1, 1, 1), (3, 1, 0), (1, 0, 0), (3, 1, 1), (1, 0, 1), (2, 0, 0), (0, 1, 0), (2, 0, 1), (0, 1, 1), (2, 1, 0), (2, 1, 1)]
    T_SENT = [(3, 0, 0), (1, 0, 0), (0, 1, 0), (3, 0, 1), (1, 0, 1), (0, 1, 1), (3, 1, 0), (1, 1, 0), (3, 1, 1), (1, 1, 1), (2, 0, 0), (2, 1, 0), (2, 0, 1), (2, 1, 1)]
    W_ORDER = [(3, 0), (1, 1), (3, 1), (1, 0), (2, 0), (0, 1), (2, 1)]

    def send_to(build, places):
        for rows, depth, side in places:
            build(2 * chip(-rows % 4, depth) + side, me).start()

    def to_all(build, order=None):
        build(partner, me).start()
        send_to(build, W_SENT if order is None else T_SENT)

    def copy(kind, source, target_buffer):
        def build(target, origin):
            return pltpu.make_async_remote_copy(
                src_ref=source.at[target],
                dst_ref=target_buffer.at[origin],
                send_sem=out_sems.at[kind, target],
                recv_sem=in_sems.at[kind, origin],
                device_id={"view": target},
                device_id_type=pl.DeviceIdType.MESH,
            )

        return build

    w_copy = copy(0, send_w, recv_w)
    t_copy = copy(1, send_t, recv_t)
    q_copy = copy(2, send_q, recv_q)
    o_copy = copy(3, send_o, recv_o)

    for load in loads[:2]:
        load.wait()
    pack_weights(gate_up, down_t, send_w)
    for load in loads[2:5]:
        load.wait()
    pack_tokens(keys, values, rates, send_t)
    for load in loads[5:]:
        load.wait()
    pack_queries(queries, send_q)
    pl.semaphore_wait(barrier, GROUP - 1)
    to_all(w_copy)
    to_all(t_copy, T_ORDER)

    own = [
        pltpu.make_async_copy(source.at[me], target.at[me], here.at[at])
        for at, (source, target) in enumerate(
            ((send_w, recv_w), (send_t, recv_t), (send_q, recv_q))
        )
    ]
    for copied in own:
        copied.start()
    clear_grads(grad)
    for copied in own:
        copied.wait()

    w_copy(partner, partner).wait_recv()
    unpack_weights(my_pair, recv_w, weight)
    for rows, depth in W_ORDER:
        pair = chip(rows, depth)
        w_copy(2 * pair, 2 * pair).wait_recv()
        w_copy(2 * pair + 1, 2 * pair + 1).wait_recv()
        unpack_weights(pair, recv_w, weight)

    def take_tokens(step):
        pair = chip(*T_ORDER[step])
        t_copy(2 * pair, 2 * pair).wait_recv()
        t_copy(2 * pair + 1, 2 * pair + 1).wait_recv()
        return pair

    t_copy(partner, partner).wait_recv()
    grad_chunk(my_pair, 0, recv_t, weight, turned, terms, grad, drain=False)
    for step in range(7):
        grad_chunk(
            take_tokens(step), 1 - step % 2, recv_t, weight, turned, terms, grad, last=step == 6
        )
        if step == 1:
            to_all(q_copy)

    renew(grad, weight, fresh, turned_down, step_sizes[me])
    gain = gain_rows[pl.ds(my_pair, 1), :]
    gain = jnp.where(my_side == 0, gain[:, :DH], gain[:, DH:])

    loop(1, GROUP, lambda step: q_copy(peer(step), peer(step)).wait_recv())
    for rows in (2, 1, 3, 0):
        block = (my_row + rows) % 4
        apply_block(block, recv_q, fresh, turned_down, gain, send_o)
        for depth in (1, 0):
            pair = chip(rows, depth)
            if rows or depth:
                o_copy(2 * pair, me).start()
                o_copy(2 * pair + 1, me).start()
    o_copy(partner, me).start()
    own_o = pltpu.make_async_copy(send_o.at[me], recv_o.at[me], here.at[3])
    own_o.start()

    def finish_sends(step):
        for build in (w_copy, t_copy, q_copy, o_copy):
            build(peer(step), me).wait_send()

    loop(1, GROUP, finish_sends)
    own_o.wait()
    half = DH // 2
    for rows in (2, 3, 1, 0):
        for depth in range(2):
            pair = chip(rows, depth)
            for side in range(2):
                if rows or depth:
                    o_copy(2 * pair + side, 2 * pair + side).wait_recv()
                elif side:
                    o_copy(partner, partner).wait_recv()
            even, odd = recv_o[2 * pair], recv_o[2 * pair + 1]
            cols = pl.ds(pl.multiple_of(pair * LANES, LANES), LANES)
            outputs[:half, cols] = side_by_side(even[:, :DH], odd[:, :DH])
            outputs[half:, cols] = side_by_side(even[:, DH:], odd[:, DH:])


def shards(keys, values, rates, queries, gate_up, down_t, step_sizes, gain):
    bf16, f32 = jnp.bfloat16, jnp.float32

    def boxes(rows):
        return [pltpu.VMEM((GROUP, rows, LANES), bf16)] * 2

    return pl.pallas_call(
        whole_kernel,
        out_shape=pltpu.VMEM(queries.shape, bf16),
        in_specs=[pl.BlockSpec(memory_space=pltpu.HBM)] * 8,
        out_specs=pl.BlockSpec(memory_space=pltpu.VMEM),
        scratch_shapes=[
            pltpu.VMEM(keys.shape, bf16),
            pltpu.VMEM(values.shape, bf16),
            pltpu.VMEM(rates.shape[::-1], bf16),
            pltpu.VMEM(queries.shape, bf16),
            pltpu.VMEM(gate_up.shape, bf16),
            pltpu.VMEM(down_t.shape, bf16),
            pltpu.SMEM(step_sizes.shape, f32),
            pltpu.VMEM((PAIRS, LANES), f32),
        ]
        + boxes(DH + DH // 2)
        + boxes(LANES)
        + boxes(DH // 2)
        + boxes(DH // 2)
        + [
            pltpu.VMEM((3, DH, HID), bf16),
            pltpu.VMEM((2, 2 * DH, 2 * LANES), bf16),
            pltpu.VMEM((2, 3, 2 * LANES, HID), bf16),
            pltpu.VMEM((3, DH, HID), f32),
            pltpu.VMEM((2, DH, HID), bf16),
            pltpu.VMEM((HID, DH), bf16),
            pltpu.SemaphoreType.DMA((4, GROUP)),
            pltpu.SemaphoreType.DMA((4, GROUP)),
            pltpu.SemaphoreType.DMA((4,)),
            pltpu.SemaphoreType.DMA((8,)),
        ],
        compiler_params=pltpu.CompilerParams(
            collective_id=0, has_side_effects=True, vmem_limit_bytes=60 << 20
        ),
    )(
        keys,
        values,
        rates.T,
        queries,
        gate_up,
        down_t,
        step_sizes,
        gain.reshape(PAIRS, LANES),
    )


def solution(mesh):
    return jax.shard_map(
        shards,
        mesh=mesh,
        in_specs=(
            P(("scene", "view"), None),
            P(("scene", "view"), None),
            P(("scene", "view"), None),
            P(("scene", "view"), None),
            P(None, None, None, "view"),
            P(None, None, "view"),
            P(),
            P(),
        ),
        out_specs=P(("scene", "view"), None),
        check_vma=False,
    )
```
